32 devices in a mesh: groups: 2 (over x), space: 16 (over z, y, core).
Axes of the slice: x: 2, y: 2, z: 4, core: 2. Of those that a mesh axis runs over, the one named last changes fastest.
Arguments:
- snapshots: float32 [24576, 2048], P(('groups', 'space')), parts along dimension 0, may hold values from -6 to 6
- block_of: int32 [512], P(('groups', 'space')), parts along dimension 0, may hold values from 0 to 7
- mass_table: float32 [8, 4, 4], replicated, as said below
Outputs:
- gram: float32 [4096, 2048], P(('groups', 'space')), parts along dimension 0
The draws below stay inside these ranges and needn't reach their ends.
There are 2 independent parts, one for each index of `groups`. The reference program is written for one: setup_inputs(seed, part) draws one part's arguments, and reference() takes and returns one part's arrays. A program takes and returns all parts, laid end to end along the dimension named above; an argument that names none is the same for every part. Nothing has to cross between parts.
Inputs may be any that keep to these rules, and one draw needn't show every extreme that they name: mass_table is symmetric; in each row the diagonal entry exceeds the sum of the other entries' magnitudes.
All inputs are finite; a program needn't handle non-finite values.
Results may differ from the reference program's by a relative error of at most 0.00005.
Values sent between devices are 32-bit elements; how exact they have to be, the bound alone decides.
No kernel may reach another device: no remote copies, remote signals or barrier semaphores. Data moves between devices by JAX's collectives and lax.ppermute only.
A program may use at most 128 MiB of HBM per device.

```python
import math
import jax
import jax.numpy as jnp
from jax import lax

S = 2048
NP = 4
FIELDS = 12
NB = 8
ELEMS = 256
VALUES = 12288


def draw_mass_table(key, part):
    key = jax.random.fold_in(key, 7)
    key_raw, key_vol, key_diag = jax.random.split(key, 3)
    raw = jnp.clip(jax.random.normal(key_raw, (NB, NP, NP), jnp.float32), -1.0, 1.0)
    volume = jnp.exp(jax.random.uniform(key_vol, (NB, 1, 1), jnp.float32, math.log(0.5), math.log(5.0)))
    symmetric = 0.6 * 0.5 * (raw + jnp.swapaxes(raw, 1, 2))
    identity = jnp.eye(NP, dtype=jnp.float32)
    diagonal = 2.0 + jax.random.uniform(key_diag, (NB, NP), jnp.float32, 0.0, 1.0)
    matrix = symmetric * (1.0 - identity) + identity * diagonal[:, :, None]
    return volume * matrix


def touch_ends(drawn, own_key, least, top_value):
    dims = drawn.shape
    index_at = [jax.random.randint(jax.random.fold_in(own_key, axis), (), 0, dims[axis]) for axis in range(len(dims))]
    drawn = drawn.at[tuple(index_at)].set(least)
    longest = dims.index(max(dims))
    index_at[longest] = (index_at[longest] + 1) % dims[longest]
    return drawn.at[tuple(index_at)].set(top_value)


def with_spikes(drawn, rng, source, target, shards_of, factor):
    owner, partner = [(jnp.arange(drawn.shape[dim]) // (drawn.shape[dim] // shards_of)).reshape([-1 if axis == dim else 1 for axis in range(drawn.ndim)]) for dim in (source, target)]
    chosen = jax.random.permutation(rng, shards_of)[partner]
    strong = (owner == chosen) | (owner == (partner + shards_of // 2) % shards_of)
    return jnp.where(strong, factor * drawn, drawn)


def steps_of(stream_key, dims, cuts, smallest, largest):
    gain, own = 1.0, jax.random.fold_in(stream_key, 6)
    for position, blocks in cuts:
        heights = jnp.exp(jax.random.uniform(jax.random.fold_in(own, position), (blocks,), jnp.float32, smallest / len(cuts), largest / len(cuts)))
        gain = gain * jnp.repeat(heights, dims[position] // blocks).reshape([-1 if axis == position else 1 for axis in range(len(dims))])
    return gain


def bell_draw_with(stream_key, extent, scale, reach, cuts, heavy, kind=jnp.bfloat16):
    array = scale * jax.random.normal(stream_key, extent, jnp.float32)
    if cuts:
        array = array * steps_of(stream_key, extent, cuts, -0.22, 0.18)
    return jnp.clip(with_spikes(array, jax.random.fold_in(stream_key, 3), *heavy), -reach, reach).astype(kind)


def setup_inputs(seed: int = 0, part: int = 0) -> dict:
    arg_keys = jax.random.split(jax.random.key(seed), 4)
    part_splits = jax.random.split(jax.random.fold_in(arg_keys[3], part), 4)
    return {
        "snapshots": bell_draw_with(part_splits[0], (VALUES, S), 1.0, 6.0, ((0, 16),), (0, 1, 16, 2.0), jnp.float32),
        "block_of": touch_ends(jax.random.randint(part_splits[1], (ELEMS,), 0, NB), jax.random.fold_in(part_splits[1], 1), 0, NB - 1).astype(jnp.int32),
        "mass_table": draw_mass_table(jax.random.fold_in(arg_keys[3], 71), part),
    }


def reference(snapshots, block_of, mass_table):
    masses = mass_table[block_of]
    grouped = snapshots.reshape(ELEMS, FIELDS, NP, S)
    weighted = jnp.einsum("eij,efjs->efis", masses, grouped, precision=lax.Precision.HIGHEST).reshape(VALUES, S)
    gram = lax.dot_general(snapshots, weighted, (((0,), (0,)), ((), ())), precision=lax.Precision.HIGHEST, preferred_element_type=jnp.float32)
    return gram / VALUES
```

```python
import functools

import jax
import jax.numpy as jnp
import numpy as np
from jax import lax
from jax.experimental import pallas as pl
from jax.experimental.pallas import tpu as pltpu
from jax.sharding import PartitionSpec as P

F32 = jnp.float32
BF16 = jnp.bfloat16
MIB = 1 << 20
CHIPS = 8
SUB = 128
TWO = 2 * SUB


def prep_kernel(scale, block_of, mass, x_hbm, xh, xl, wh, wl, x, table, dh, dl, sems):
    rows, order = x_hbm.shape
    classes, nodes = mass.shape[0], mass.shape[1]
    per_element = rows // block_of.shape[0]
    band = dh.shape[0]
    wide = order // 2
    copies = []
    for b in range(rows // band):
        for h in range(2):
            at = (pl.ds(b * band, band), pl.ds(h * wide, wide))
            copy = pltpu.make_async_copy(x_hbm.at[at], x.at[at], sems.at[2 * b + h])
            copy.start()
            copies.append(copy)
    row = lax.broadcasted_iota(jnp.int32, (8, band), 0)
    column = lax.broadcasted_iota(jnp.int32, (8, band), 1)
    for k in range(classes):
        tile = jnp.zeros((8, band), F32)
        for i in range(nodes):
            for j in range(nodes):
                here = (row % nodes == i) & (column % nodes == j)
                tile = jnp.where(here, mass[k, i, j] * scale, tile)
        table[8 * k : 8 * k + 8, :] = tile
    for b in range(rows // band):
        for g in range(band // 8):
            kind = block_of[(b * band + 8 * g) // per_element]
            tile = table[pl.ds(pl.multiple_of(kind * 8, 8), 8), :]
            tile = jnp.where((row + 8 * g) // nodes == column // nodes, tile, 0.0)
            high = tile.astype(BF16).astype(F32)
            dh[8 * g : 8 * g + 8, :] = high
            dl[8 * g : 8 * g + 8, :] = tile - high
        mh, ml = dh[...].astype(BF16), dl[...].astype(BF16)
        for h in range(2):
            copies[2 * b + h].wait()

            @pl.loop(0, wide // TWO)
            def _(t):
                at = (pl.ds(b * band, band), pl.ds(pl.multiple_of(h * wide + t * TWO, TWO), TWO))
                value = x[at]
                high = value.astype(BF16)
                low = (value - high.astype(F32)).astype(BF16)
                xh[at] = high
                xl[at] = low
                dot = functools.partial(jnp.dot, preferred_element_type=F32)
                weighted = dot(mh, high) + dot(mh, low) + dot(ml, high)
                high = weighted.astype(BF16)
                wh[at] = high
                wl[at] = (weighted - high.astype(F32)).astype(BF16)


def prepare(snapshots, block_of, mass_table, scale):
    rows, order = snapshots.shape
    band = TWO
    smem = pl.BlockSpec(memory_space=pltpu.SMEM)
    vmem = pl.BlockSpec(memory_space=pltpu.VMEM)
    return pl.pallas_call(
        functools.partial(prep_kernel, scale),
        out_shape=[pltpu.VMEM((rows, order), BF16)] * 4,
        in_specs=[smem, smem, pl.BlockSpec(memory_space=pl.ANY)],
        out_specs=[vmem] * 4,
        scratch_shapes=[
            pltpu.VMEM((rows, order), F32),
            pltpu.VMEM((8 * mass_table.shape[0], band), F32),
            pltpu.VMEM((band, band), F32),
            pltpu.VMEM((band, band), F32),
            pltpu.SemaphoreType.DMA((2 * (rows // band),)),
        ],
        compiler_params=pltpu.CompilerParams(vmem_limit_bytes=32 * MIB),
        cost_estimate=pl.CostEstimate(
            flops=6 * rows * order * band, bytes_accessed=6 * rows * order, transcendentals=0
        ),
        name="weighting",
    )(block_of, mass_table, snapshots)


WIDTHS = (5 * SUB, 4 * SUB)
LHS, K0, K1, K2, K3, K4A, K4B = range(7)
INSTANCES = {name: 7 * i for i, name in enumerate(("1A", "1B", "2A", "2B", "3A", "3B", "4A", "4B", "5"))}
CORE, R1, R2, R3, R4 = range(63, 68)
TABLE = 68


def ring_chip(p):
    p %= CHIPS
    return 2 * p if p < 4 else 2 * (CHIPS - 1 - p) + 1


def ring_device(p, core):
    return 2 * ring_chip(p) + core


def fourth(q, r):
    return r if q % CHIPS < 4 else 1 - r


def position_table():
    table = np.zeros((2 * CHIPS, TABLE), np.int32)

    def strip(q, half=None):
        at = TWO * ring_chip(q)
        cols = [TWO * ring_chip(q + k) for k in range(5)]
        fours = [cols[4] + SUB * fourth(q, r) for r in range(2)]
        if half is None:
            return [at] + cols[:4] + fours
        return [at + SUB * half] + cols[:4] + [fours[half]] * 2

    for p in range(CHIPS):
        for c in range(2):
            sign = 1 - 2 * c
            row = strip(p + 4, c) + strip(p + 4, 1 - c)
            for step in (2, 3, 4):
                row += strip(p + sign * (5 - step)) + strip(p - sign * (5 - step))
            row += strip(p)
            row += [SUB * c] + [TWO * ring_chip(p - k) for k in (1, 2, 3)]
            row += [TWO * ring_chip(p + 4) + SUB * (c if (p + 4) % CHIPS < 4 else 1 - c)]
            table[ring_device(p, c)] = row
    return table


def product(xh, xl, wh, wl, rows, at, width):
    def dot(a, b):
        return lax.dot_general(
            a[:, rows], b[:, pl.ds(at, width)], (((0,), (0,)), ((), ())), preferred_element_type=F32
        )

    return dot(xh, wh) + dot(xh, wl) + dot(xl, wh)


def strip_kernel(base, part, height, names, table, xh, xl, wh, wl, *refs):
    ins, out = refs[:-1], refs[-1]

    def entry(i):
        return pl.multiple_of(table[base + i], SUB)

    def put(r, n, c, w, value):
        for name, ref in zip(names, ins):
            if name == "same":
                value = value + ref[r : r + n, c : c + w]
        out[r : r + n, c : c + w] = value

    lhs = entry(LHS)
    c = 0
    if part == 0:
        for r in range(height // SUB):
            rows = pl.ds(pl.multiple_of(lhs + SUB * r, SUB), SUB)
            put(SUB * r, SUB, 0, SUB, product(xh, xl, wh, wl, rows, entry(K4A + r), SUB))
        c = SUB
    for k in (K3, K2) if part == 0 else (K1, K0):
        put(0, height, c, TWO, product(xh, xl, wh, wl, pl.ds(lhs, height), entry(k), TWO))
        c += TWO
    for name, ref in zip(names, ins):
        if name == "half":
            rows = pl.ds(pl.multiple_of(table[CORE], SUB), SUB)
            out[rows, :] = out[rows, :] + ref[...]


def strip(name, part, height, operands, table, same=(), half=()):
    width = WIDTHS[part]
    names = ("same",) * len(same) + ("half",) * len(half)
    vmem = pl.BlockSpec(memory_space=pltpu.VMEM)
    depth = operands[0].shape[0]
    pinned = [pltpu.with_memory_space_constraint(x, pltpu.VMEM) for x in operands]
    return pl.pallas_call(
        functools.partial(strip_kernel, INSTANCES[name], part, height, names),
        out_shape=jax.ShapeDtypeStruct((height, width), F32),
        in_specs=[pl.BlockSpec(memory_space=pltpu.SMEM)] + [vmem] * (4 + len(names)),
        out_specs=vmem,
        compiler_params=pltpu.CompilerParams(vmem_limit_bytes=20 * MIB),
        cost_estimate=pl.CostEstimate(
            flops=6 * height * width * depth,
            bytes_accessed=4 * height * width * (1 + len(names)),
            transcendentals=0,
        ),
        name=f"strip_{name}_{part}",
    )(table, *pinned, *same, *half)


def total_kernel(part, table, mine, other, own, *sends):
    core = pl.multiple_of(table[CORE], SUB)
    rows = pl.ds(core, SUB)
    own[...] = mine[rows, :] + other[rows, :]
    if part == 0:
        sends[0][...] = own[:, 0:SUB]
    at = (SUB, SUB + TWO) if part == 0 else (0,)
    for out, c in zip(sends[1:] if part == 0 else sends, at):
        columns = pl.ds(pl.multiple_of(core + c, SUB), SUB)
        out[...] = mine[:, columns] + other[:, columns]


def total(part, table, mine, other):
    vmem = pl.BlockSpec(memory_space=pltpu.VMEM)
    blocks = [(SUB, WIDTHS[part])]
    blocks += [(SUB, SUB), (TWO, SUB), (TWO, SUB)] if part == 0 else [(TWO, SUB)]
    return pl.pallas_call(
        functools.partial(total_kernel, part),
        out_shape=[jax.ShapeDtypeStruct(b, F32) for b in blocks],
        in_specs=[pl.BlockSpec(memory_space=pltpu.SMEM), vmem, vmem],
        out_specs=[vmem] * len(blocks),
        compiler_params=pltpu.CompilerParams(vmem_limit_bytes=20 * MIB),
        name=f"total_{part}",
    )(table, mine, other)


def place_kernel(table, own0, own1, r4, r3, r2, r1, out):
    def put(entry, width, value):
        out[:, pl.ds(pl.multiple_of(table[entry], SUB), width)] = value

    base = INSTANCES["5"]
    core = table[CORE] // SUB
    for r in range(2):

        @pl.when(core == r)
        def _():
            put(base + K4A + r, SUB, own0[:, 0:SUB])

    put(base + K3, TWO, own0[:, SUB : SUB + TWO])
    put(base + K2, TWO, own0[:, SUB + TWO :])
    put(base + K1, TWO, own1[:, 0:TWO])
    put(base + K0, TWO, own1[:, TWO:])
    put(R4, SUB, r4[...].T)
    put(R3, TWO, r3[...].T)
    put(R2, TWO, r2[...].T)
    put(R1, TWO, r1[...].T)


def place(table, *parts, order):
    vmem = pl.BlockSpec(memory_space=pltpu.VMEM)
    return pl.pallas_call(
        place_kernel,
        out_shape=jax.ShapeDtypeStruct((SUB, order), F32),
        in_specs=[pl.BlockSpec(memory_space=pltpu.SMEM)] + [vmem] * len(parts),
        out_specs=vmem,
        compiler_params=pltpu.CompilerParams(vmem_limit_bytes=20 * MIB),
        name="place",
    )(table, *parts)


def ring_gram(snapshots, block_of, mass_table, axis):
    rows, order = snapshots.shape
    ring, swap, fours = [], [], []
    far = {1: [], 2: [], 3: []}
    for p in range(CHIPS):
        for c in range(2):
            here = ring_device(p, c)
            ring.append((here, ring_device(p + 1 - 2 * c, c)))
            swap.append((here, ring_device(p, 1 - c)))
            fours.append((here, ring_device(p + 4, fourth(p, c))))
            for k in far:
                far[k].append((here, ring_device(p + k, c)))
    table = jnp.asarray(position_table())[lax.axis_index(axis)]
    operands = prepare(snapshots, block_of, mass_table, 1.0 / (rows * 2 * CHIPS))
    send = lambda x, pairs: lax.ppermute(x, axis, pairs)

    moving = [None, None]
    for part in range(2):
        other = send(strip("1B", part, SUB, operands, table), swap)
        moving[part] = strip("1A", part, SUB, operands, table, same=(other,))
    for step in ("2", "3", "4"):
        for part in range(2):
            other = send(strip(step + "B", part, TWO, operands, table), swap)
            came = send(moving[part], ring)
            same, half = ((other,), (came,)) if step == "2" else ((other, came), ())
            moving[part] = strip(step + "A", part, TWO, operands, table, same=same, half=half)
    own, got = [], []
    for part in range(2):
        came = send(moving[part], ring)
        mine = strip("5", part, TWO, operands, table, same=(came,))
        outs = total(part, table, mine, send(mine, swap))
        own.append(outs[0])
        if part == 0:
            got += [send(outs[1], fours), send(outs[2], far[3]), send(outs[3], far[2])]
        else:
            got += [send(outs[1], far[1])]
    return place(table, *own, *got, order=order)


def scattered_gram(snapshots, block_of, mass_table, axis):
    rows, order = snapshots.shape
    xh, xl, wh, wl = prepare(snapshots, block_of, mass_table, 1.0 / (rows * lax.axis_size(axis)))

    def dot(a, b):
        return lax.dot_general(a, b, (((0,), (0,)), ((), ())), preferred_element_type=F32)

    return lax.psum_scatter(
        dot(xh, wh) + (dot(xh, wl) + dot(xl, wh)), axis, scatter_dimension=0, tiled=True
    )


def per_device(snapshots, block_of, mass_table):
    axis = "space"
    ring = lax.axis_size(axis) == 2 * CHIPS and snapshots.shape[1] == 2 * CHIPS * SUB
    form = ring_gram if ring else scattered_gram
    return form(snapshots, block_of, mass_table, axis)


def solution(mesh):
    return jax.shard_map(
        per_device,
        mesh=mesh,
        in_specs=(P(("groups", "space"), None), P(("groups", "space")), P()),
        out_specs=P(("groups", "space"), None),
        check_vma=False,
    )
```

```python
import functools

import jax
import jax.numpy as jnp
import numpy as np
from jax import lax
from jax.experimental import pallas as pl
from jax.experimental.pallas import tpu as pltpu
from jax.sharding import PartitionSpec as P

F32 = jnp.float32
BF16 = jnp.bfloat16
MIB = 1 << 20
CHIPS = 8
SUB = 128
TWO = 2 * SUB


def prep_kernel(scale, block_hbm, mass_hbm, x_hbm, xh, xl, wh, wl, x, table, both, block_of, mass, sems, small):
    rows, order = x_hbm.shape
    nodes, _, classes = mass.shape
    first = [pltpu.make_async_copy(block_hbm, block_of, small.at[0]), pltpu.make_async_copy(mass_hbm, mass, small.at[1])]
    for copy in first:
        copy.start()
    per_element = rows // block_of.shape[0]
    bands, _, band = both.shape
    wide = order // PIECES
    copies = []
    for b in range(bands):
        for h in range(PIECES):
            at = (pl.ds(b * band, band), pl.ds(h * wide, wide))
            copy = pltpu.make_async_copy(x_hbm.at[at], x.at[at], sems.at[PIECES * b + h])
            copy.start()
            copies.append(copy)
    for copy in first:
        copy.wait()
    row = lax.broadcasted_iota(jnp.int32, (8, band), 0)
    column = lax.broadcasted_iota(jnp.int32, (8, band), 1)
    here = [[(row % nodes == i) & (column % nodes == j) for j in range(nodes)] for i in range(nodes)]
    for k in range(classes):
        tile = jnp.zeros((8, band), F32)
        for i in range(nodes):
            for j in range(nodes):
                tile = jnp.where(here[i][j], mass[i, j, k] * scale, tile)
        table[8 * k : 8 * k + 8, :] = tile
    for b in range(bands):
        for g in range(0, band // 8, 2):
            tiles = []
            for e in (g, g + 1):
                kind = block_of[(b * band + 8 * e) // per_element]
                tile = table[pl.ds(pl.multiple_of(kind * 8, 8), 8), :]
                tiles.append(jnp.where((row + 8 * e) // nodes == column // nodes, tile, 0.0))
            tile = jnp.concatenate(tiles, axis=0)
            high = tile.astype(BF16)
            both[b, 8 * g : 8 * g + 16, :] = high
            both[b, band + 8 * g : band + 8 * g + 16, :] = (tile - high.astype(F32)).astype(BF16)
    dot = functools.partial(jnp.dot, preferred_element_type=F32)
    for b in range(bands):
        for h in range(PIECES):
            copies[PIECES * b + h].wait()
            at = (pl.ds(b * band, band), pl.ds(h * wide, wide))
            value = x[at]
            high = value.astype(BF16)
            low = (value - high.astype(F32)).astype(BF16)
            xh[at] = high
            xl[at] = low
            weighted = dot(both[b], high)
            weighted = weighted[:band] + weighted[band:] + dot(both[b, :band], low)
            high = weighted.astype(BF16)
            wh[at] = high
            wl[at] = (weighted - high.astype(F32)).astype(BF16)


PIECES = 1


def prepare(snapshots, block_of, mass_table, scale):
    rows, order = snapshots.shape
    band = TWO
    bands = rows // band
    smem = pl.BlockSpec(memory_space=pltpu.SMEM)
    vmem = pl.BlockSpec(memory_space=pltpu.VMEM)
    return pl.pallas_call(
        functools.partial(prep_kernel, scale),
        out_shape=[pltpu.VMEM((rows, order), BF16)] * 4,
        in_specs=[pl.BlockSpec(memory_space=pl.ANY)] * 3,
        out_specs=[vmem] * 4,
        scratch_shapes=[
            pltpu.VMEM((rows, order), F32),
            pltpu.VMEM((8 * mass_table.shape[0], band), F32),
            pltpu.VMEM((bands, 2 * band, band), BF16),
            pltpu.SMEM(block_of.shape, jnp.int32),
            pltpu.SMEM(mass_table.shape[1:] + mass_table.shape[:1], F32),
            pltpu.SemaphoreType.DMA((PIECES * bands,)),
            pltpu.SemaphoreType.DMA((2,)),
        ],
        compiler_params=pltpu.CompilerParams(vmem_limit_bytes=32 * MIB),
        cost_estimate=pl.CostEstimate(
            flops=6 * rows * order * band, bytes_accessed=6 * rows * order, transcendentals=0
        ),
        name="weighting",
    )(*(pltpu.with_memory_space_constraint(x, pltpu.HBM) for x in (block_of, mass_table.transpose(1, 2, 0), snapshots)))


LHS, K0, K1, K2, K3, K4A, K4B = range(7)
FAR, NEAR = (K4A, K3, K2), (K1, K0)
FULL = FAR + NEAR
COST = 5000000000.0
COSTS = {'strip_4A_far': 0.02, 'strip_4A_near': 10, 'strip_5_far': 0.02, 'strip_5_near': 3, 'total_far': 0.1, 'total_near': 0.02, 'add_own': 0.02, 'place_far': 3}
CHAIN = 1
INSTANCES = {name: 7 * i for i, name in enumerate(("1A", "1B", "2A", "2B", "3A", "3B", "4A", "4B", "5"))}
CORE, R1, R2, R3, R4, FOUR = range(63, 69)
TABLE = 69


def ring_chip(p):
    p %= CHIPS
    return 2 * p if p < 4 else 2 * (CHIPS - 1 - p) + 1


def ring_device(p, core):
    return 2 * ring_chip(p) + core


def pair(q, k):
    return q + (((2, 1, -1), (-2, 3, -3))[q % 2][k - 1])


def fourth(q, r):
    return r if q % CHIPS < 4 else 1 - r


def position_table():
    table = np.zeros((2 * CHIPS, TABLE), np.int32)

    def strip(q, half=None):
        at = TWO * ring_chip(q)
        cols = [TWO * ring_chip(pair(q, k) if k else q) for k in range(4)]
        fours = [TWO * ring_chip(q + 4) + SUB * fourth(q, r) for r in range(2)]
        if half is None:
            return [at] + cols + fours
        return [at + SUB * half] + cols + [fours[half]] * 2

    for p in range(CHIPS):
        for c in range(2):
            sign = 1 - 2 * c
            row = strip(p + 4, c) + strip(p + 4, 1 - c)
            for step in (2, 3, 4):
                row += strip(p + sign * (5 - step)) + strip(p - sign * (5 - step))
            row += strip(p)
            row += [SUB * c] + [TWO * ring_chip(q) for k in (1, 2, 3) for q in range(CHIPS) if pair(q, k) % CHIPS == p]
            row += [TWO * ring_chip(p + 4) + SUB * (c if (p + 4) % CHIPS < 4 else 1 - c)]
            row += [strip(p, c)[K4A]]
            table[ring_device(p, c)] = row
    return table


def width_of(k):
    return SUB if k == K4A else TWO


def in_order(kernel, out_shape, operands, spaces, after, name, **kwargs):
    if after is not None:
        operands, spaces = operands + [after], spaces + [pl.ANY]
        inner, count = kernel, len(operands)
        kernel = lambda *refs: inner(*refs[: count - 1], *refs[count:])
    outs = pl.pallas_call(
        kernel,
        out_shape=out_shape,
        in_specs=[pl.BlockSpec(memory_space=s) for s in spaces],
        out_specs=[pl.BlockSpec(memory_space=pltpu.VMEM)] * len(out_shape),
        compiler_params=pltpu.CompilerParams(vmem_limit_bytes=20 * MIB),
        cost_estimate=pl.CostEstimate(flops=int(COST * COSTS.get(name, 1)), bytes_accessed=0, transcendentals=0),
        name=name,
        **kwargs,
    )(*operands)
    return list(outs)


def strip_kernel(base, height, group, names, table, xh, xl, wh, wl, *refs):
    ins, out = refs[:-1], refs[-1]

    def entry(i):
        return pl.multiple_of(table[base + i], SUB)

    def dot(a, b):
        return jnp.dot(a, b, preferred_element_type=F32)

    rows = pl.ds(entry(LHS), height)
    ah, al = xh[:, rows].T, xl[:, rows].T
    c = 0
    for k in group:
        w = width_of(k)
        pieces = [(0, height, entry(k))]
        if k == K4A:
            pieces = [(SUB * r, SUB, entry(K4A + r)) for r in range(height // SUB)]
        for r, n, at in pieces:
            bh, bl = wh[:, pl.ds(at, w)], wl[:, pl.ds(at, w)]
            lh, ll = ah[r : r + n], al[r : r + n]
            value = dot(lh, bh) + dot(lh, bl) + dot(ll, bh)
            for name, ref in zip(names, ins):
                if name == "same":
                    c0 = ref.shape[1] - out.shape[1] + c if group == NEAR else c
                    value = value + ref[r : r + n, c0 : c0 + w]
            out[r : r + n, c : c + w] = value
        c += w
    for name, ref in zip(names, ins):
        if name == "half":
            rows = pl.ds(pl.multiple_of(table[CORE], SUB), SUB)
            out[rows, :] = out[rows, :] + ref[...]


def strip(name, group, height, operands, table, after, same=(), half=()):
    names = ("same",) * len(same) + ("half",) * len(half)
    pinned = [pltpu.with_memory_space_constraint(x, pltpu.VMEM) for x in operands]
    return in_order(
        functools.partial(strip_kernel, INSTANCES[name], height, group, names),
        [jax.ShapeDtypeStruct((height, sum(map(width_of, group))), F32)],
        [pltpu.with_memory_space_constraint(table, pltpu.SMEM), *pinned, *same, *half],
        [pltpu.SMEM] + [pltpu.VMEM] * (4 + len(names)),
        after,
        name=f"strip_{name}" + ("" if group == FULL else "_far" if group == FAR else "_near"),
    )[0]


def sum_kernel(own, came, out):
    out[...] = own[:, own.shape[1] - out.shape[1] :] + came[...]


def add_own(own, came, after):
    return in_order(
        sum_kernel,
        [jax.ShapeDtypeStruct(came.shape, F32)],
        [own, came],
        [pltpu.VMEM] * 2,
        after,
        name="add_own",
    )[0]


def total_kernel(far, table, *refs):
    terms, own, sends = (refs[:4], refs[4], refs[5:]) if far else (refs[:2], refs[2], refs[3:])
    core = pl.multiple_of(table[CORE], SUB)

    def add(rows, at, n):
        values = [ref[rows, pl.ds(at, n)] for ref in terms]
        return (values[0] + values[1]) + (values[2] + values[3]) if far else values[0] + values[1]

    own[...] = add(pl.ds(core, SUB), 0, own.shape[1])
    if far:
        sends[0][...] = own[:, 0:SUB]
    at = (SUB, SUB + TWO) if far else (0,)
    for out, c0 in zip(sends[1:] if far else sends, at):
        out[...] = add(slice(None), pl.multiple_of(core + c0, SUB), SUB)


def total(far, table, after, *terms):
    blocks = [(SUB, terms[-1].shape[1])]
    blocks += [(SUB, SUB), (TWO, SUB), (TWO, SUB)] if far else [(TWO, SUB)]
    return in_order(
        functools.partial(total_kernel, far),
        [jax.ShapeDtypeStruct(b, F32) for b in blocks],
        [pltpu.with_memory_space_constraint(table, pltpu.SMEM), *terms],
        [pltpu.SMEM] + [pltpu.VMEM] * len(terms),
        after,
        name="total_far" if far else "total_near",
    )


def place_kernel(far, table, *refs):
    own, *got = refs[: 4 if far else 2]
    out, turned, sems = refs[-3:]
    base = INSTANCES["5"]
    copies = []

    def put(entry, source):
        columns = pl.ds(pl.multiple_of(table[entry], SUB), source.shape[1])
        copy = pltpu.make_async_copy(source, out.at[:, columns], sems.at[len(copies)])
        copy.start()
        copies.append(copy)

    if far:
        put(FOUR, own.at[:, 0:SUB])
    c = SUB if far else 0
    for k in (K3, K2) if far else (K1, K0):
        put(base + k, own.at[:, c : c + TWO])
        c += TWO
    c = 0
    for entry, ref in zip((R4, R3, R2) if far else (R1,), got):
        w = ref.shape[0]
        turned[:, c : c + w] = ref[...].T
        put(entry, turned.at[:, c : c + w])
        c += w
    for copy in copies:
        copy.wait()


def place(table, rest, own, *got, order, after):
    far = rest is None
    name = "place_far" if far else "place_near"
    operands = [pltpu.with_memory_space_constraint(table, pltpu.SMEM), own, *got]
    spaces = [pltpu.SMEM] + [pltpu.VMEM] * (1 + len(got))
    kernel, aliases = functools.partial(place_kernel, far), {}
    if not far:
        operands, spaces, aliases = operands + [rest], spaces + [pl.ANY], {len(operands): 0}
    if after is not None:
        operands, spaces = operands + [after], spaces + [pl.ANY]
    return pl.pallas_call(
        kernel,
        out_shape=jax.ShapeDtypeStruct((SUB, order), F32),
        in_specs=[pl.BlockSpec(memory_space=s) for s in spaces],
        out_specs=pl.BlockSpec(memory_space=pl.ANY),
        scratch_shapes=[
            pltpu.VMEM((SUB, sum(g.shape[0] for g in got)), F32),
            pltpu.SemaphoreType.DMA((6,)),
        ],
        input_output_aliases=aliases,
        compiler_params=pltpu.CompilerParams(vmem_limit_bytes=20 * MIB),
        cost_estimate=pl.CostEstimate(flops=int(COST * COSTS.get(name, 1)), bytes_accessed=0, transcendentals=0),
        name=name,
    )(*operands)


def ring_gram(snapshots, block_of, mass_table, axis):
    rows, order = snapshots.shape
    ring, swap, fours = [], [], []
    far = {1: [], 2: [], 3: []}
    for p in range(CHIPS):
        for c in range(2):
            here = ring_device(p, c)
            ring.append((here, ring_device(p + 1 - 2 * c, c)))
            swap.append((here, ring_device(p, 1 - c)))
            fours.append((here, ring_device(p + 4, fourth(p, c))))
            for k in far:
                far[k].append((here, ring_device(pair(p, k), c)))
    table = jnp.asarray(position_table())[lax.axis_index(axis)]
    operands = prepare(snapshots, block_of, mass_table, 1.0 / (rows * 2 * CHIPS))
    send = lambda x, pairs: lax.ppermute(x, axis, pairs)
    compute = lambda name, group, height, *rest, **adds: strip(
        name, group, height, operands, table, *rest, **adds
    )

    b = compute("1B", FULL, SUB, None)
    o = send(b, swap)
    last = compute("2B", FULL, TWO, b)
    o2 = send(last, swap)
    a_far = compute("1A", FAR, SUB, last, same=(o,))
    last = compute("1A", NEAR, SUB, a_far, same=(o,))
    r_far, r_near = send(a_far, ring), send(last, ring)
    o = o2
    for step in (2, 3, 4):
        if step < 4:
            last = b = compute(f"{step + 1}B", FULL, TWO, last)
        elif CHAIN == 3:
            last = b = compute("5", FAR, TWO, last)
        after_far = ((o,), (r_far,)) if step == 2 else ((o, r_far), ())
        last = a_far = compute(f"{step}A", FAR, TWO, last, *after_far)
        if step == 4 and CHAIN == 1:
            last = b = compute("5", FAR, TWO, last)
        after_near = ((o,), (r_near,)) if step == 2 else ((o, r_near), ())
        last = a_near = compute(f"{step}A", NEAR, TWO, last, *after_near)
        if step == 4 and CHAIN == 2:
            last = b = compute("5", FAR, TWO, last)
        r_far, r_near = send(a_far, ring), send(a_near, ring)
        o = send(b, swap)
    last = b_near = compute("5", NEAR, TWO, last)
    own_far, *sends = total(True, table, last, b, o, r_far, send(r_far, swap))
    got = [send(sends[0], fours), send(sends[1], far[3]), send(sends[2], far[2])]
    near = add_own(b_near, r_near, own_far)
    own_near, sent = total(False, table, None, near, send(near, swap))
    got_near = send(sent, far[1])
    out = place(table, None, own_far, *got, order=order, after=own_near)
    return place(table, out, own_near, got_near, order=order, after=None)


def scattered_gram(snapshots, block_of, mass_table, axis):
    rows, order = snapshots.shape
    xh, xl, wh, wl = prepare(snapshots, block_of, mass_table, 1.0 / (rows * lax.axis_size(axis)))

    def dot(a, b):
        return lax.dot_general(a, b, (((0,), (0,)), ((), ())), preferred_element_type=F32)

    return lax.psum_scatter(
        dot(xh, wh) + (dot(xh, wl) + dot(xl, wh)), axis, scatter_dimension=0, tiled=True
    )


def per_device(snapshots, block_of, mass_table):
    axis = "space"
    ring = lax.axis_size(axis) == 2 * CHIPS and snapshots.shape[1] == 2 * CHIPS * SUB
    form = ring_gram if ring else scattered_gram
    return form(snapshots, block_of, mass_table, axis)


def solution(mesh):
    return jax.shard_map(
        per_device,
        mesh=mesh,
        in_specs=(P(("groups", "space"), None), P(("groups", "space")), P()),
        out_specs=P(("groups", "space"), None),
        check_vma=False,
    )
```

```python
import functools

import jax
import jax.numpy as jnp
import numpy as np
from jax import lax
from jax.experimental import pallas as pl
from jax.experimental.pallas import tpu as pltpu
from jax.sharding import PartitionSpec as P

F32 = jnp.float32
BF16 = jnp.bfloat16
MIB = 1 << 20
CHIPS = 8
SUB = 128
TWO = 2 * SUB


def prep_kernel(scale, block_hbm, mass_hbm, x_hbm, xh, xl, wh, wl, x, table, both, block_of, mass, sems, small):
    rows, order = x_hbm.shape
    nodes, _, classes = mass.shape
    first = [pltpu.make_async_copy(block_hbm, block_of, small.at[0]), pltpu.make_async_copy(mass_hbm, mass, small.at[1])]
    for copy in first:
        copy.start()
    per_element = rows // block_of.shape[0]
    bands, _, band = both.shape
    wide = order // PIECES
    copies = []
    for b in range(bands):
        for h in range(PIECES):
            at = (pl.ds(b * band, band), pl.ds(h * wide, wide))
            copy = pltpu.make_async_copy(x_hbm.at[at], x.at[at], sems.at[PIECES * b + h])
            copy.start()
            copies.append(copy)
    for copy in first:
        copy.wait()
    row = lax.broadcasted_iota(jnp.int32, (8, band), 0)
    column = lax.broadcasted_iota(jnp.int32, (8, band), 1)
    here = [[(row % nodes == i) & (column % nodes == j) for j in range(nodes)] for i in range(nodes)]
    for k in range(classes):
        tile = jnp.zeros((8, band), F32)
        for i in range(nodes):
            for j in range(nodes):
                tile = jnp.where(here[i][j], mass[i, j, k] * scale, tile)
        table[8 * k : 8 * k + 8, :] = tile
    for b in range(bands):
        for g in range(0, band // 8, 2):
            tiles = []
            for e in (g, g + 1):
                kind = block_of[(b * band + 8 * e) // per_element]
                tile = table[pl.ds(pl.multiple_of(kind * 8, 8), 8), :]
                tiles.append(jnp.where((row + 8 * e) // nodes == column // nodes, tile, 0.0))
            tile = jnp.concatenate(tiles, axis=0)
            high = tile.astype(BF16)
            both[b, 8 * g : 8 * g + 16, :] = high
            both[b, band + 8 * g : band + 8 * g + 16, :] = (tile - high.astype(F32)).astype(BF16)
    dot = functools.partial(jnp.dot, preferred_element_type=F32)
    for b in range(bands):
        for h in range(PIECES):
            copies[PIECES * b + h].wait()
            at = (pl.ds(b * band, band), pl.ds(h * wide, wide))
            value = x[at]
            high = value.astype(BF16)
            low = (value - high.astype(F32)).astype(BF16)
            xh[at] = high
            xl[at] = low
            weighted = dot(both[b], high)
            weighted = weighted[:band] + weighted[band:] + dot(both[b, :band], low)
            high = weighted.astype(BF16)
            wh[at] = high
            wl[at] = (weighted - high.astype(F32)).astype(BF16)


PIECES = 1


def prepare(snapshots, block_of, mass_table, scale):
    rows, order = snapshots.shape
    band = TWO
    bands = rows // band
    smem = pl.BlockSpec(memory_space=pltpu.SMEM)
    vmem = pl.BlockSpec(memory_space=pltpu.VMEM)
    return pl.pallas_call(
        functools.partial(prep_kernel, scale),
        out_shape=[pltpu.VMEM((rows, order), BF16)] * 4,
        in_specs=[pl.BlockSpec(memory_space=pl.ANY)] * 3,
        out_specs=[vmem] * 4,
        scratch_shapes=[
            pltpu.VMEM((rows, order), F32),
            pltpu.VMEM((8 * mass_table.shape[0], band), F32),
            pltpu.VMEM((bands, 2 * band, band), BF16),
            pltpu.SMEM(block_of.shape, jnp.int32),
            pltpu.SMEM(mass_table.shape[1:] + mass_table.shape[:1], F32),
            pltpu.SemaphoreType.DMA((PIECES * bands,)),
            pltpu.SemaphoreType.DMA((2,)),
        ],
        compiler_params=pltpu.CompilerParams(vmem_limit_bytes=32 * MIB),
        cost_estimate=pl.CostEstimate(
            flops=6 * rows * order * band, bytes_accessed=6 * rows * order, transcendentals=0
        ),
        name="weighting",
    )(*(pltpu.with_memory_space_constraint(x, pltpu.HBM) for x in (block_of, mass_table.transpose(1, 2, 0), snapshots)))


LHS, K0, K1, K2, K3, K4A, K4B = range(7)
FAR, NEAR = (K4A, K3, K2), (K1, K0)
FULL = FAR + NEAR
COST = 5000000000.0
COSTS = {'strip_4A_far': 0.02, 'strip_4A_near': 10, 'strip_5_far': 0.02, 'strip_5_near': 3, 'total_far': 0.1, 'total_near': 0.02, 'add_own': 0.02, 'place_far': 3}
CHAIN = 1
INSTANCES = {name: 7 * i for i, name in enumerate(("1A", "1B", "2A", "2B", "3A", "3B", "4A", "4B", "5"))}
CORE, R1, R2, R3, R4, FOUR = range(63, 69)
TABLE = 69


def ring_chip(p):
    p %= CHIPS
    return 2 * p if p < 4 else 2 * (CHIPS - 1 - p) + 1


def ring_device(p, core):
    return 2 * ring_chip(p) + core


PAIRS = ((7, 3, 0, 2, 5, 6, 4, 1), (1, 2, 5, 6, 3, 7, 0, 4), (5, 6, 4, 0, 1, 3, 7, 2))


def pair(q, k):
    return PAIRS[k - 1][q % CHIPS]


def fourth(q, r):
    return r if q % CHIPS < 4 else 1 - r


def position_table():
    table = np.zeros((2 * CHIPS, TABLE), np.int32)

    def strip(q, half=None):
        at = TWO * ring_chip(q)
        cols = [TWO * ring_chip(pair(q, k) if k else q) for k in range(4)]
        fours = [TWO * ring_chip(q + 4) + SUB * fourth(q, r) for r in range(2)]
        if half is None:
            return [at] + cols + fours
        return [at + SUB * half] + cols + [fours[half]] * 2

    for p in range(CHIPS):
        for c in range(2):
            sign = 1 - 2 * c
            row = strip(p + 4, c) + strip(p + 4, 1 - c)
            for step in (2, 3, 4):
                row += strip(p + sign * (5 - step)) + strip(p - sign * (5 - step))
            row += strip(p)
            row += [SUB * c] + [TWO * ring_chip(q) for k in (1, 2, 3) for q in range(CHIPS) if pair(q, k) % CHIPS == p]
            row += [TWO * ring_chip(p + 4) + SUB * (c if (p + 4) % CHIPS < 4 else 1 - c)]
            row += [strip(p, c)[K4A]]
            table[ring_device(p, c)] = row
    return table


def width_of(k):
    return SUB if k == K4A else TWO


def in_order(kernel, out_shape, operands, spaces, after, name, **kwargs):
    if after is not None:
        operands, spaces = operands + [after], spaces + [pl.ANY]
        inner, count = kernel, len(operands)
        kernel = lambda *refs: inner(*refs[: count - 1], *refs[count:])
    outs = pl.pallas_call(
        kernel,
        out_shape=out_shape,
        in_specs=[pl.BlockSpec(memory_space=s) for s in spaces],
        out_specs=[pl.BlockSpec(memory_space=pltpu.VMEM)] * len(out_shape),
        compiler_params=pltpu.CompilerParams(vmem_limit_bytes=20 * MIB),
        cost_estimate=pl.CostEstimate(flops=int(COST * COSTS.get(name, 1)), bytes_accessed=0, transcendentals=0),
        name=name,
        **kwargs,
    )(*operands)
    return list(outs)


def strip_kernel(base, height, group, names, table, xh, xl, wh, wl, *refs):
    ins, out = refs[:-1], refs[-1]

    def entry(i):
        return pl.multiple_of(table[base + i], SUB)

    def dot(a, b):
        return jnp.dot(a, b, preferred_element_type=F32)

    rows = pl.ds(entry(LHS), height)
    ah, al = xh[:, rows].T, xl[:, rows].T
    c = 0
    for k in group:
        w = width_of(k)
        pieces = [(0, height, entry(k))]
        if k == K4A:
            pieces = [(SUB * r, SUB, entry(K4A + r)) for r in range(height // SUB)]
        for r, n, at in pieces:
            bh, bl = wh[:, pl.ds(at, w)], wl[:, pl.ds(at, w)]
            lh, ll = ah[r : r + n], al[r : r + n]
            value = dot(lh, bh) + dot(lh, bl) + dot(ll, bh)
            for name, ref in zip(names, ins):
                if name == "same":
                    c0 = ref.shape[1] - out.shape[1] + c if group == NEAR else c
                    value = value + ref[r : r + n, c0 : c0 + w]
            out[r : r + n, c : c + w] = value
        c += w
    for name, ref in zip(names, ins):
        if name == "half":
            rows = pl.ds(pl.multiple_of(table[CORE], SUB), SUB)
            out[rows, :] = out[rows, :] + ref[...]


def strip(name, group, height, operands, table, after, same=(), half=()):
    names = ("same",) * len(same) + ("half",) * len(half)
    pinned = [pltpu.with_memory_space_constraint(x, pltpu.VMEM) for x in operands]
    return in_order(
        functools.partial(strip_kernel, INSTANCES[name], height, group, names),
        [jax.ShapeDtypeStruct((height, sum(map(width_of, group))), F32)],
        [pltpu.with_memory_space_constraint(table, pltpu.SMEM), *pinned, *same, *half],
        [pltpu.SMEM] + [pltpu.VMEM] * (4 + len(names)),
        after,
        name=f"strip_{name}" + ("" if group == FULL else "_far" if group == FAR else "_near"),
    )[0]


def sum_kernel(own, came, out):
    out[...] = own[:, own.shape[1] - out.shape[1] :] + came[...]


def add_own(own, came, after):
    return in_order(
        sum_kernel,
        [jax.ShapeDtypeStruct(came.shape, F32)],
        [own, came],
        [pltpu.VMEM] * 2,
        after,
        name="add_own",
    )[0]


def total_kernel(far, table, *refs):
    terms, own, sends = (refs[:4], refs[4], refs[5:]) if far else (refs[:2], refs[2], refs[3:])
    core = pl.multiple_of(table[CORE], SUB)

    def add(rows, at, n):
        values = [ref[rows, pl.ds(at, n)] for ref in terms]
        return (values[0] + values[1]) + (values[2] + values[3]) if far else values[0] + values[1]

    own[...] = add(pl.ds(core, SUB), 0, own.shape[1])
    if far:
        sends[0][...] = own[:, 0:SUB]
    at = (SUB, SUB + TWO) if far else (0,)
    for out, c0 in zip(sends[1:] if far else sends, at):
        out[...] = add(slice(None), pl.multiple_of(core + c0, SUB), SUB)


def total(far, table, after, *terms):
    blocks = [(SUB, terms[-1].shape[1])]
    blocks += [(SUB, SUB), (TWO, SUB), (TWO, SUB)] if far else [(TWO, SUB)]
    return in_order(
        functools.partial(total_kernel, far),
        [jax.ShapeDtypeStruct(b, F32) for b in blocks],
        [pltpu.with_memory_space_constraint(table, pltpu.SMEM), *terms],
        [pltpu.SMEM] + [pltpu.VMEM] * len(terms),
        after,
        name="total_far" if far else "total_near",
    )


SENT = {K4A: 4, K3: 3, K2: 2, K1: 1}


def place_kernel(table, far, near, *refs):
    got, (out, turned, sems) = refs[: len(SENT)], refs[len(SENT) :]
    copies = []

    def put(entry, source):
        columns = pl.ds(pl.multiple_of(table[entry], SUB), source.shape[1])
        copy = pltpu.make_async_copy(source, out.at[:, columns], sems.at[len(copies)])
        copy.start()
        copies.append(copy)

    for group, own in ((FAR, far), (NEAR, near)):
        c = 0
        for k in group:
            put(FOUR if k == K4A else INSTANCES["5"] + k, own.at[:, c : c + width_of(k)])
            c += width_of(k)
    c = 0
    for k, ref in zip(SENT, got):
        w = ref.shape[0]
        turned[:, c : c + w] = ref[...].T
        put(R1 + SENT[k] - 1, turned.at[:, c : c + w])
        c += w
    for copy in copies:
        copy.wait()


def place(table, far, near, *got, order):
    return pl.pallas_call(
        place_kernel,
        out_shape=jax.ShapeDtypeStruct((SUB, order), F32),
        in_specs=[pl.BlockSpec(memory_space=pltpu.SMEM)]
        + [pl.BlockSpec(memory_space=pltpu.VMEM)] * (2 + len(got)),
        out_specs=pl.BlockSpec(memory_space=pl.ANY),
        scratch_shapes=[
            pltpu.VMEM((SUB, sum(g.shape[0] for g in got)), F32),
            pltpu.SemaphoreType.DMA((9,)),
        ],
        compiler_params=pltpu.CompilerParams(vmem_limit_bytes=20 * MIB),
        cost_estimate=pl.CostEstimate(flops=int(COST), bytes_accessed=0, transcendentals=0),
        name="place",
    )(pltpu.with_memory_space_constraint(table, pltpu.SMEM), far, near, *got)


def ring_gram(snapshots, block_of, mass_table, axis):
    rows, order = snapshots.shape
    ring, swap, fours = [], [], []
    far = {1: [], 2: [], 3: []}
    for p in range(CHIPS):
        for c in range(2):
            here = ring_device(p, c)
            ring.append((here, ring_device(p + 1 - 2 * c, c)))
            swap.append((here, ring_device(p, 1 - c)))
            fours.append((here, ring_device(p + 4, fourth(p, c))))
            for k in far:
                far[k].append((here, ring_device(pair(p, k), c)))
    table = jnp.asarray(position_table())[lax.axis_index(axis)]
    operands = prepare(snapshots, block_of, mass_table, 1.0 / (rows * 2 * CHIPS))
    send = lambda x, pairs: lax.ppermute(x, axis, pairs)
    compute = lambda name, group, height, *rest, **adds: strip(
        name, group, height, operands, table, *rest, **adds
    )

    b = compute("1B", FULL, SUB, None)
    o = send(b, swap)
    last = compute("2B", FULL, TWO, b)
    o2 = send(last, swap)
    a_far = compute("1A", FAR, SUB, last, same=(o,))
    last = compute("1A", NEAR, SUB, a_far, same=(o,))
    r_far, r_near = send(a_far, ring), send(last, ring)
    o = o2
    for step in (2, 3, 4):
        if step < 4:
            last = b = compute(f"{step + 1}B", FULL, TWO, last)
        elif CHAIN == 3:
            last = b = compute("5", FAR, TWO, last)
        after_far = ((o,), (r_far,)) if step == 2 else ((o, r_far), ())
        last = a_far = compute(f"{step}A", FAR, TWO, last, *after_far)
        if step == 4 and CHAIN == 1:
            last = b = compute("5", FAR, TWO, last)
        after_near = ((o,), (r_near,)) if step == 2 else ((o, r_near), ())
        last = a_near = compute(f"{step}A", NEAR, TWO, last, *after_near)
        if step == 4 and CHAIN == 2:
            last = b = compute("5", FAR, TWO, last)
        r_far, r_near = send(a_far, ring), send(a_near, ring)
        o = send(b, swap)
    last = b_near = compute("5", NEAR, TWO, last)
    own_far, *sends = total(True, table, last, b, o, r_far, send(r_far, swap))
    got = [send(sends[0], fours), send(sends[1], far[3]), send(sends[2], far[2])]
    near = add_own(b_near, r_near, own_far)
    own_near, sent = total(False, table, None, near, send(near, swap))
    got_near = send(sent, far[1])
    return place(table, own_far, own_near, *got, got_near, order=order)


def scattered_gram(snapshots, block_of, mass_table, axis):
    rows, order = snapshots.shape
    xh, xl, wh, wl = prepare(snapshots, block_of, mass_table, 1.0 / (rows * lax.axis_size(axis)))

    def dot(a, b):
        return lax.dot_general(a, b, (((0,), (0,)), ((), ())), preferred_element_type=F32)

    return lax.psum_scatter(
        dot(xh, wh) + (dot(xh, wl) + dot(xl, wh)), axis, scatter_dimension=0, tiled=True
    )


def per_device(snapshots, block_of, mass_table):
    axis = "space"
    ring = lax.axis_size(axis) == 2 * CHIPS and snapshots.shape[1] == 2 * CHIPS * SUB
    form = ring_gram if ring else scattered_gram
    return form(snapshots, block_of, mass_table, axis)


def solution(mesh):
    return jax.shard_map(
        per_device,
        mesh=mesh,
        in_specs=(P(("groups", "space"), None), P(("groups", "space")), P()),
        out_specs=P(("groups", "space"), None),
        check_vma=False,
    )
```

```python
import functools

import jax
import jax.numpy as jnp
import numpy as np
from jax import lax
from jax.experimental import pallas as pl
from jax.experimental.pallas import tpu as pltpu
from jax.sharding import PartitionSpec as P

F32 = jnp.float32
BF16 = jnp.bfloat16
MIB = 1 << 20
CHIPS = 8
SUB = 128
TWO = 2 * SUB


def prep_kernel(scale, block_hbm, mass_hbm, x_hbm, xh, xl, wh, wl, x, table, both, block_of, mass, sems, small):
    rows, order = x_hbm.shape
    nodes, _, classes = mass.shape
    first = [pltpu.make_async_copy(block_hbm, block_of, small.at[0]), pltpu.make_async_copy(mass_hbm, mass, small.at[1])]
    for copy in first:
        copy.start()
    per_element = rows // block_of.shape[0]
    bands, _, band = both.shape
    wide = order // PIECES
    copies = []
    for b in range(bands):
        for h in range(PIECES):
            at = (pl.ds(b * band, band), pl.ds(h * wide, wide))
            copy = pltpu.make_async_copy(x_hbm.at[at], x.at[at], sems.at[PIECES * b + h])
            copy.start()
            copies.append(copy)
    for copy in first:
        copy.wait()
    row = lax.broadcasted_iota(jnp.int32, (8, band), 0)
    column = lax.broadcasted_iota(jnp.int32, (8, band), 1)
    here = [[(row % nodes == i) & (column % nodes == j) for j in range(nodes)] for i in range(nodes)]
    for k in range(classes):
        tile = jnp.zeros((8, band), F32)
        for i in range(nodes):
            for j in range(nodes):
                tile = jnp.where(here[i][j], mass[i, j, k] * scale, tile)
        table[8 * k : 8 * k + 8, :] = tile
    for b in range(bands):
        for g in range(0, band // 8, 2):
            tiles = []
            for e in (g, g + 1):
                kind = block_of[(b * band + 8 * e) // per_element]
                tile = table[pl.ds(pl.multiple_of(kind * 8, 8), 8), :]
                tiles.append(jnp.where((row + 8 * e) // nodes == column // nodes, tile, 0.0))
            tile = jnp.concatenate(tiles, axis=0)
            high = tile.astype(BF16)
            both[b, 8 * g : 8 * g + 16, :] = high
            both[b, band + 8 * g : band + 8 * g + 16, :] = (tile - high.astype(F32)).astype(BF16)
    dot = functools.partial(jnp.dot, preferred_element_type=F32)
    for b in range(bands):
        for h in range(PIECES):
            copies[PIECES * b + h].wait()
            at = (pl.ds(b * band, band), pl.ds(h * wide, wide))
            value = x[at]
            high = value.astype(BF16)
            low = (value - high.astype(F32)).astype(BF16)
            xh[at] = high
            xl[at] = low
            weighted = dot(both[b], high)
            weighted = weighted[:band] + weighted[band:] + dot(both[b, :band], low)
            high = weighted.astype(BF16)
            wh[at] = high
            wl[at] = (weighted - high.astype(F32)).astype(BF16)


PIECES = 1


def prepare(snapshots, block_of, mass_table, scale):
    rows, order = snapshots.shape
    band = TWO
    bands = rows // band
    smem = pl.BlockSpec(memory_space=pltpu.SMEM)
    vmem = pl.BlockSpec(memory_space=pltpu.VMEM)
    return pl.pallas_call(
        functools.partial(prep_kernel, scale),
        out_shape=[pltpu.VMEM((rows, order), BF16)] * 4,
        in_specs=[pl.BlockSpec(memory_space=pl.ANY)] * 3,
        out_specs=[vmem] * 4,
        scratch_shapes=[
            pltpu.VMEM((rows, order), F32),
            pltpu.VMEM((8 * mass_table.shape[0], band), F32),
            pltpu.VMEM((bands, 2 * band, band), BF16),
            pltpu.SMEM(block_of.shape, jnp.int32),
            pltpu.SMEM(mass_table.shape[1:] + mass_table.shape[:1], F32),
            pltpu.SemaphoreType.DMA((PIECES * bands,)),
            pltpu.SemaphoreType.DMA((2,)),
        ],
        compiler_params=pltpu.CompilerParams(vmem_limit_bytes=32 * MIB),
        cost_estimate=pl.CostEstimate(
            flops=6 * rows * order * band, bytes_accessed=6 * rows * order, transcendentals=0
        ),
        name="weighting",
    )(*(pltpu.with_memory_space_constraint(x, pltpu.HBM) for x in (block_of, mass_table.transpose(1, 2, 0), snapshots)))


LHS, K0, K1, K2, K3, K4A, K4B = range(7)
FAR, NEAR = (K4A, K3, K2), (K1, K0)
FULL = FAR + NEAR
COST = 5000000000.0
COSTS = {"sum_4_far": 0.02, "sum_4_near": 10, "strip_5_far": 0.02, "strip_5_near": 3, "total_far": 0.1, "total_near": 0.02, "add_own": 0.02}
INSTANCES = {name: 7 * i for i, name in enumerate(("1A", "1B", "2A", "2B", "3A", "3B", "4A", "4B", "5"))}
CORE, R1, R2, R3, R4, FOUR = range(63, 69)
TABLE = 69


def ring_chip(p):
    p %= CHIPS
    return 2 * p if p < 4 else 2 * (CHIPS - 1 - p) + 1


def ring_device(p, core):
    return 2 * ring_chip(p) + core


PAIRS = ((7, 3, 0, 2, 5, 6, 4, 1), (1, 2, 5, 6, 3, 7, 0, 4), (5, 6, 4, 0, 1, 3, 7, 2))


def pair(q, k):
    return PAIRS[k - 1][q % CHIPS]


def fourth(q, r):
    return r if q % CHIPS < 4 else 1 - r


def position_table():
    table = np.zeros((2 * CHIPS, TABLE), np.int32)

    def strip(q, half=None):
        at = TWO * ring_chip(q)
        cols = [TWO * ring_chip(pair(q, k) if k else q) for k in range(4)]
        fours = [TWO * ring_chip(q + 4) + SUB * fourth(q, r) for r in range(2)]
        if half is None:
            return [at] + cols + fours
        return [at + SUB * half] + cols + [fours[half]] * 2

    for p in range(CHIPS):
        for c in range(2):
            sign = 1 - 2 * c
            row = strip(p + 4, c) + strip(p + 4, 1 - c)
            for step in (2, 3, 4):
                row += strip(p + sign * (5 - step)) + strip(p - sign * (5 - step))
            row += strip(p)
            row += [SUB * c] + [TWO * ring_chip(q) for k in (1, 2, 3) for q in range(CHIPS) if pair(q, k) % CHIPS == p]
            row += [TWO * ring_chip(p + 4) + SUB * (c if (p + 4) % CHIPS < 4 else 1 - c)]
            row += [strip(p, c)[K4A]]
            table[ring_device(p, c)] = row
    return table


PACKED = ((K1, 0, 0, TWO, 0), (K1, SUB, 0, TWO, TWO), (K0, 0, 0, TWO, 2 * TWO), (K0, SUB, SUB, SUB, 3 * TWO))
PACKED_SHAPE = (SUB, 3 * TWO + SUB)


def near_column(k, c):
    return c if k == K1 else TWO + c


def width_of(k):
    return SUB if k == K4A else TWO


def in_order(kernel, out_shape, operands, spaces, after, name, **kwargs):
    if after is not None:
        operands, spaces = operands + [after], spaces + [pl.ANY]
        inner, count = kernel, len(operands)
        kernel = lambda *refs: inner(*refs[: count - 1], *refs[count:])
    outs = pl.pallas_call(
        kernel,
        out_shape=out_shape,
        in_specs=[pl.BlockSpec(memory_space=s) for s in spaces],
        out_specs=[pl.BlockSpec(memory_space=pltpu.VMEM)] * len(out_shape),
        compiler_params=pltpu.CompilerParams(vmem_limit_bytes=20 * MIB),
        cost_estimate=pl.CostEstimate(flops=int(COST * COSTS.get(name, 1)), bytes_accessed=0, transcendentals=0),
        name=name,
        **kwargs,
    )(*operands)
    return list(outs)


def strip_kernel(base, height, group, names, pack, table, xh, xl, wh, wl, *refs):
    ins, out = refs[:-1], refs[-1]
    width = sum(map(width_of, group))

    def entry(i):
        return pl.multiple_of(table[base + i], SUB)

    def dot(a, b):
        return jnp.dot(a, b, preferred_element_type=F32)

    rows = pl.ds(entry(LHS), height)
    ah, al = xh[:, rows].T, xl[:, rows].T
    c = 0
    for k in group:
        w = width_of(k)
        pieces = [(0, height, entry(k))]
        if k == K4A:
            pieces = [(SUB * r, SUB, entry(K4A + r)) for r in range(height // SUB)]
        for r, n, at in pieces:
            bh, bl = wh[:, pl.ds(at, w)], wl[:, pl.ds(at, w)]
            lh, ll = ah[r : r + n], al[r : r + n]
            value = dot(lh, bh) + dot(lh, bl) + dot(ll, bh)
            for name, ref in zip(names, ins):
                if name == "same":
                    c0 = ref.shape[1] - width + c if group == NEAR else c
                    value = value + ref[r : r + n, c0 : c0 + w]
            if not pack:
                out[r : r + n, c : c + w] = value
        if pack:
            for _, r, c0, n, at in (p for p in PACKED if p[0] == k):
                out[:, at : at + n] = value[r : r + SUB, c0 : c0 + n]
        c += w
    for name, ref in zip(names, ins):
        if name == "half" and pack:
            for mine in range(2):

                @pl.when(table[CORE] == SUB * mine)
                def _():
                    for k, r, c0, n, at in PACKED:
                        if r == SUB * mine:
                            c = near_column(k, c0)
                            out[:, at : at + n] = out[:, at : at + n] + ref[:, c : c + n]

        elif name == "half":
            rows = pl.ds(pl.multiple_of(table[CORE], SUB), SUB)
            out[rows, :] = out[rows, :] + ref[...]


def strip(name, group, height, operands, table, after, same=(), half=(), pack=False):
    names = ("same",) * len(same) + ("half",) * len(half)
    pinned = [pltpu.with_memory_space_constraint(x, pltpu.VMEM) for x in operands]
    return in_order(
        functools.partial(strip_kernel, INSTANCES[name], height, group, names, pack),
        [jax.ShapeDtypeStruct(PACKED_SHAPE if pack else (height, sum(map(width_of, group))), F32)],
        [pltpu.with_memory_space_constraint(table, pltpu.SMEM), *pinned, *same, *half],
        [pltpu.SMEM] + [pltpu.VMEM] * (4 + len(names)),
        after,
        name=f"strip_{name}" + ("" if group == FULL else "_far" if group == FAR else "_near"),
    )[0]


def sum_kernel(group, *refs):
    *olds, came, out = refs
    if group == FAR:
        value = came[...]
        for ref in olds:
            value = value + ref[:, : out.shape[1]]
        out[...] = value
        return
    for k, r, c0, n, at in PACKED:
        value = came[:, at : at + n]
        for ref in olds:
            c = ref.shape[1] - 2 * TWO + near_column(k, c0)
            value = value + ref[r : r + SUB, c : c + n]
        out[:, at : at + n] = value


def add_up(name, group, after, came, *olds):
    return in_order(
        functools.partial(sum_kernel, group),
        [jax.ShapeDtypeStruct(came.shape, F32)],
        [*olds, came],
        [pltpu.VMEM] * (1 + len(olds)),
        after,
        name=name,
    )[0]


def total_far_kernel(table, a, b, c, d, own, four, *sends):
    core = pl.multiple_of(table[CORE], SUB)

    def add(rows, columns):
        return (a[rows, columns] + b[rows, columns]) + (c[rows, columns] + d[rows, columns])

    own[...] = add(pl.ds(core, SUB), slice(None))
    four[...] = own[:, 0:SUB]
    for out, at in zip(sends, (SUB, SUB + TWO)):
        out[...] = add(slice(None), pl.ds(pl.multiple_of(core + at, SUB), SUB))


def total_near_kernel(table, a, b, own, sent):
    core = pl.multiple_of(table[CORE], SUB)

    def add(at, n):
        columns = pl.ds(at, n)
        return a[:, columns] + b[:, columns]

    own[:, 0:TWO] = add(pl.multiple_of(2 * core, SUB), TWO)
    for r in range(2):
        sent[SUB * r : SUB * r + SUB, :] = add(pl.multiple_of(TWO * r + core, SUB), SUB)

    @pl.when(core == 0)
    def _():
        own[:, TWO:] = add(2 * TWO, TWO)

    @pl.when(core != 0)
    def _():
        own[:, TWO : TWO + SUB] = add(2 * TWO + SUB, SUB).T
        own[:, TWO + SUB :] = add(3 * TWO, SUB)


def total(group, table, after, *terms):
    blocks = [(SUB, sum(map(width_of, group)))]
    blocks += [(SUB, SUB), (TWO, SUB), (TWO, SUB)] if group == FAR else [(TWO, SUB)]
    return in_order(
        total_far_kernel if group == FAR else total_near_kernel,
        [jax.ShapeDtypeStruct(b, F32) for b in blocks],
        [pltpu.with_memory_space_constraint(table, pltpu.SMEM), *terms],
        [pltpu.SMEM] + [pltpu.VMEM] * len(terms),
        after,
        name="total_far" if group == FAR else "total_near",
    )


SENT = {K4A: 4, K3: 3, K2: 2, K1: 1}


def place_kernel(table, far, near, *refs):
    got, (out, turned, sems) = refs[: len(SENT)], refs[len(SENT) :]
    copies = []

    def put(entry, source):
        columns = pl.ds(pl.multiple_of(table[entry], SUB), source.shape[1])
        copy = pltpu.make_async_copy(source, out.at[:, columns], sems.at[len(copies)])
        copy.start()
        copies.append(copy)

    for group, own in ((FAR, far), (NEAR, near)):
        c = 0
        for k in group:
            put(FOUR if k == K4A else INSTANCES["5"] + k, own.at[:, c : c + width_of(k)])
            c += width_of(k)
    c = 0
    for k, ref in zip(SENT, got):
        w = ref.shape[0]
        turned[:, c : c + w] = ref[...].T
        put(R1 + SENT[k] - 1, turned.at[:, c : c + w])
        c += w
    for copy in copies:
        copy.wait()


def place(table, far, near, *got, order):
    return pl.pallas_call(
        place_kernel,
        out_shape=jax.ShapeDtypeStruct((SUB, order), F32),
        in_specs=[pl.BlockSpec(memory_space=pltpu.SMEM)]
        + [pl.BlockSpec(memory_space=pltpu.VMEM)] * (2 + len(got)),
        out_specs=pl.BlockSpec(memory_space=pl.ANY),
        scratch_shapes=[
            pltpu.VMEM((SUB, sum(g.shape[0] for g in got)), F32),
            pltpu.SemaphoreType.DMA((9,)),
        ],
        compiler_params=pltpu.CompilerParams(vmem_limit_bytes=20 * MIB),
        cost_estimate=pl.CostEstimate(flops=int(COST), bytes_accessed=0, transcendentals=0),
        name="place",
    )(pltpu.with_memory_space_constraint(table, pltpu.SMEM), far, near, *got)


def ring_gram(snapshots, block_of, mass_table, axis):
    rows, order = snapshots.shape
    ring, swap, fours = [], [], []
    far = {1: [], 2: [], 3: []}
    for p in range(CHIPS):
        for c in range(2):
            here = ring_device(p, c)
            ring.append((here, ring_device(p + 1 - 2 * c, c)))
            swap.append((here, ring_device(p, 1 - c)))
            fours.append((here, ring_device(p + 4, fourth(p, c))))
            for k in far:
                far[k].append((here, ring_device(pair(p, k), c)))
    table = jnp.asarray(position_table())[lax.axis_index(axis)]
    operands = prepare(snapshots, block_of, mass_table, 1.0 / (rows * 2 * CHIPS))
    send = lambda x, pairs: lax.ppermute(x, axis, pairs)
    compute = lambda name, group, height, *rest, **adds: strip(
        name, group, height, operands, table, *rest, **adds
    )

    b = compute("1B", FULL, SUB, None)
    o = send(b, swap)
    last = compute("2B", FULL, TWO, b)
    o2 = send(last, swap)
    a_far = compute("1A", FAR, SUB, last, same=(o,))
    last = compute("1A", NEAR, SUB, a_far, same=(o,))
    r_far, r_near = send(a_far, ring), send(last, ring)
    o = o2
    for step in (2, 3, 4):
        if step < 4:
            last = b = compute(f"{step + 1}B", FULL, TWO, last)
        if step == 2:
            last = a_far = compute("2A", FAR, TWO, last, same=(o,), half=(r_far,))
            last = a_near = compute("2A", NEAR, TWO, last, same=(o,), half=(r_near,), pack=True)
        else:
            last = mine = compute(f"{step}A", FULL, TWO, last)
            last = a_far = add_up(f"sum_{step}_far", FAR, last, r_far, mine, o)
            if step == 4:
                last = b = compute("5", FAR, TWO, last)
            last = a_near = add_up(f"sum_{step}_near", NEAR, last, r_near, mine, o)
        r_far, r_near = send(a_far, ring), send(a_near, ring)
        o = send(b, swap)
    last = b_near = compute("5", NEAR, TWO, last)
    own_far, *sends = total(FAR, table, last, b, o, r_far, send(r_far, swap))
    got = [send(sends[0], fours), send(sends[1], far[3]), send(sends[2], far[2])]
    near = add_up("add_own", NEAR, own_far, r_near, b_near)
    own_near, sent = total(NEAR, table, None, near, send(near, swap))
    got_near = send(sent, far[1])
    return place(table, own_far, own_near, *got, got_near, order=order)


def scattered_gram(snapshots, block_of, mass_table, axis):
    rows, order = snapshots.shape
    xh, xl, wh, wl = prepare(snapshots, block_of, mass_table, 1.0 / (rows * lax.axis_size(axis)))

    def dot(a, b):
        return lax.dot_general(a, b, (((0,), (0,)), ((), ())), preferred_element_type=F32)

    return lax.psum_scatter(
        dot(xh, wh) + (dot(xh, wl) + dot(xl, wh)), axis, scatter_dimension=0, tiled=True
    )


def per_device(snapshots, block_of, mass_table):
    axis = "space"
    ring = lax.axis_size(axis) == 2 * CHIPS and snapshots.shape[1] == 2 * CHIPS * SUB
    form = ring_gram if ring else scattered_gram
    return form(snapshots, block_of, mass_table, axis)


def solution(mesh):
    return jax.shard_map(
        per_device,
        mesh=mesh,
        in_specs=(P(("groups", "space"), None), P(("groups", "space")), P()),
        out_specs=P(("groups", "space"), None),
        check_vma=False,
    )
```

```python
import functools

import jax
import jax.numpy as jnp
import numpy as np
from jax import lax
from jax.experimental import pallas as pl
from jax.experimental.pallas import tpu as pltpu
from jax.sharding import PartitionSpec as P

F32 = jnp.float32
BF16 = jnp.bfloat16
MIB = 1 << 20
CHIPS = 8
SUB = 128
TWO = 2 * SUB


def prep_kernel(scale, axis, block_hbm, mass_hbm, x_hbm, places, xh, xl, wh, wl, place, x, table, both, block_of, mass, sems, small):
    rows, order = x_hbm.shape
    nodes, _, classes = mass.shape
    pairs = ((block_hbm, block_of), (mass_hbm, mass), (places.at[lax.axis_index(axis)], place))
    first = [pltpu.make_async_copy(a, b, small.at[i]) for i, (a, b) in enumerate(pairs)]
    for copy in first:
        copy.start()
    per_element = rows // block_of.shape[0]
    bands, _, band = both.shape
    wide = order // PIECES
    copies = []
    for b in range(bands):
        for h in range(PIECES):
            at = (pl.ds(b * band, band), pl.ds(h * wide, wide))
            copy = pltpu.make_async_copy(x_hbm.at[at], x.at[at], sems.at[PIECES * b + h])
            copy.start()
            copies.append(copy)
    for copy in first:
        copy.wait()
    row = lax.broadcasted_iota(jnp.int32, (8, band), 0)
    column = lax.broadcasted_iota(jnp.int32, (8, band), 1)
    here = [[(row % nodes == i) & (column % nodes == j) for j in range(nodes)] for i in range(nodes)]
    for k in range(classes):
        tile = jnp.zeros((8, band), F32)
        for i in range(nodes):
            for j in range(nodes):
                tile = jnp.where(here[i][j], mass[i, j, k] * scale, tile)
        table[8 * k : 8 * k + 8, :] = tile
    for b in range(bands):
        for g in range(0, band // 8, 2):
            tiles = []
            for e in (g, g + 1):
                kind = block_of[(b * band + 8 * e) // per_element]
                tile = table[pl.ds(pl.multiple_of(kind * 8, 8), 8), :]
                tiles.append(jnp.where((row + 8 * e) // nodes == column // nodes, tile, 0.0))
            tile = jnp.concatenate(tiles, axis=0)
            high = tile.astype(BF16)
            both[b, 8 * g : 8 * g + 16, :] = high
            both[b, band + 8 * g : band + 8 * g + 16, :] = (tile - high.astype(F32)).astype(BF16)
    dot = functools.partial(jnp.dot, preferred_element_type=F32)
    for b in range(bands):
        for h in range(PIECES):
            copies[PIECES * b + h].wait()
            at = (pl.ds(b * band, band), pl.ds(h * wide, wide))
            value = x[at]
            high = value.astype(BF16)
            low = (value - high.astype(F32)).astype(BF16)
            xh[at] = high
            xl[at] = low
            weighted = dot(both[b], high)
            weighted = weighted[:band] + weighted[band:] + dot(both[b, :band], low)
            high = weighted.astype(BF16)
            wh[at] = high
            wl[at] = (weighted - high.astype(F32)).astype(BF16)


PIECES = 1


def prepare(snapshots, block_of, mass_table, scale, places, axis):
    rows, order = snapshots.shape
    band = TWO
    bands = rows // band
    smem = pl.BlockSpec(memory_space=pltpu.SMEM)
    vmem = pl.BlockSpec(memory_space=pltpu.VMEM)
    return pl.pallas_call(
        functools.partial(prep_kernel, scale, axis),
        out_shape=[pltpu.VMEM((rows, order), BF16)] * 4 + [pltpu.SMEM(places.shape[1:], jnp.int32)],
        in_specs=[pl.BlockSpec(memory_space=pl.ANY)] * 4,
        out_specs=[vmem] * 4 + [smem],
        scratch_shapes=[
            pltpu.VMEM((rows, order), F32),
            pltpu.VMEM((8 * mass_table.shape[0], band), F32),
            pltpu.VMEM((bands, 2 * band, band), BF16),
            pltpu.SMEM(block_of.shape, jnp.int32),
            pltpu.SMEM(mass_table.shape[1:] + mass_table.shape[:1], F32),
            pltpu.SemaphoreType.DMA((PIECES * bands,)),
            pltpu.SemaphoreType.DMA((3,)),
        ],
        compiler_params=pltpu.CompilerParams(vmem_limit_bytes=32 * MIB),
        cost_estimate=pl.CostEstimate(
            flops=6 * rows * order * band, bytes_accessed=6 * rows * order, transcendentals=0
        ),
        name="weighting",
    )(*(pltpu.with_memory_space_constraint(x, pltpu.HBM) for x in (block_of, mass_table.transpose(1, 2, 0), snapshots, places)))


LHS, K0, K1, K2, K3, K4A, K4B = range(7)
FAR, NEAR = (K4A, K3, K2), (K1, K0)
FULL = FAR + NEAR
COST = 5000000000.0
COSTS = {"sum_4_far": 0.02, "sum_4_near": 10, "strip_5_far": 0.02, "strip_5_near": 3, "total_far": 0.1, "total_near": 0.02, "add_own": 0.02}
INSTANCES = {name: 7 * i for i, name in enumerate(("1A", "1B", "2A", "2B", "3A", "3B", "4A", "4B", "5"))}
CORE, R1, R2, R3, R4, FOUR = range(63, 69)


def ring_chip(p):
    p %= CHIPS
    return 2 * p if p < 4 else 2 * (CHIPS - 1 - p) + 1


def ring_device(p, core):
    return 2 * ring_chip(p) + core


PAIRS = ((7, 3, 0, 2, 5, 6, 4, 1), (1, 2, 5, 6, 3, 7, 0, 4), (5, 6, 4, 0, 1, 3, 7, 2))


def pair(q, k):
    return PAIRS[k - 1][q % CHIPS]


def fourth(q, r):
    return r if q % CHIPS < 4 else 1 - r


def position_table():
    table = np.zeros((2 * CHIPS, 1, 128), np.int32)

    def strip(q, half=None):
        at = TWO * ring_chip(q)
        cols = [TWO * ring_chip(pair(q, k) if k else q) for k in range(4)]
        fours = [TWO * ring_chip(q + 4) + SUB * fourth(q, r) for r in range(2)]
        if half is None:
            return [at] + cols + fours
        return [at + SUB * half] + cols + [fours[half]] * 2

    for p in range(CHIPS):
        for c in range(2):
            sign = 1 - 2 * c
            row = strip(p + 4, c) + strip(p + 4, 1 - c)
            for step in (2, 3, 4):
                row += strip(p + sign * (5 - step)) + strip(p - sign * (5 - step))
            row += strip(p)
            row += [SUB * c] + [TWO * ring_chip(q) for k in (1, 2, 3) for q in range(CHIPS) if pair(q, k) % CHIPS == p]
            row += [TWO * ring_chip(p + 4) + SUB * (c if (p + 4) % CHIPS < 4 else 1 - c)]
            row += [strip(p, c)[K4A]]
            table[ring_device(p, c), 0, : len(row)] = row
    return table


PACKED = ((K1, 0, 0, TWO, 0), (K1, SUB, 0, TWO, TWO), (K0, 0, 0, TWO, 2 * TWO), (K0, SUB, SUB, SUB, 3 * TWO))
PACKED_SHAPE = (SUB, 3 * TWO + SUB)


def near_column(k, c):
    return c if k == K1 else TWO + c


def width_of(k):
    return SUB if k == K4A else TWO


def in_order(kernel, out_shape, operands, spaces, after, name, **kwargs):
    if after is not None:
        operands, spaces = operands + [after], spaces + [pl.ANY]
        inner, count = kernel, len(operands)
        kernel = lambda *refs: inner(*refs[: count - 1], *refs[count:])
    outs = pl.pallas_call(
        kernel,
        out_shape=out_shape,
        in_specs=[pl.BlockSpec(memory_space=s) for s in spaces],
        out_specs=[pl.BlockSpec(memory_space=pltpu.VMEM)] * len(out_shape),
        compiler_params=pltpu.CompilerParams(vmem_limit_bytes=20 * MIB),
        cost_estimate=pl.CostEstimate(flops=int(COST * COSTS.get(name, 1)), bytes_accessed=0, transcendentals=0),
        name=name,
        **kwargs,
    )(*operands)
    return list(outs)


def strip_kernel(base, height, group, names, pack, table, xh, xl, wh, wl, *refs):
    ins, out = refs[:-1], refs[-1]
    width = sum(map(width_of, group))

    def entry(i):
        return pl.multiple_of(table[0, base + i], SUB)

    def dot(a, b):
        return jnp.dot(a, b, preferred_element_type=F32)

    rows = pl.ds(entry(LHS), height)
    ah, al = xh[:, rows].T, xl[:, rows].T
    c = 0
    for k in group:
        w = width_of(k)
        pieces = [(0, height, entry(k))]
        if k == K4A:
            pieces = [(SUB * r, SUB, entry(K4A + r)) for r in range(height // SUB)]
        for r, n, at in pieces:
            bh, bl = wh[:, pl.ds(at, w)], wl[:, pl.ds(at, w)]
            lh, ll = ah[r : r + n], al[r : r + n]
            value = dot(lh, bh) + dot(lh, bl) + dot(ll, bh)
            for name, ref in zip(names, ins):
                if name == "same":
                    c0 = ref.shape[1] - width + c if group == NEAR else c
                    value = value + ref[r : r + n, c0 : c0 + w]
            if not pack:
                out[r : r + n, c : c + w] = value
        if pack:
            for _, r, c0, n, at in (p for p in PACKED if p[0] == k):
                out[:, at : at + n] = value[r : r + SUB, c0 : c0 + n]
        c += w
    for name, ref in zip(names, ins):
        if name == "half" and pack:
            for mine in range(2):

                @pl.when(table[0, CORE] == SUB * mine)
                def _():
                    for k, r, c0, n, at in PACKED:
                        if r == SUB * mine:
                            c = near_column(k, c0)
                            out[:, at : at + n] = out[:, at : at + n] + ref[:, c : c + n]

        elif name == "half":
            rows = pl.ds(pl.multiple_of(table[0, CORE], SUB), SUB)
            out[rows, :] = out[rows, :] + ref[...]


def strip(name, group, height, operands, table, after, same=(), half=(), pack=False):
    names = ("same",) * len(same) + ("half",) * len(half)
    pinned = [pltpu.with_memory_space_constraint(x, pltpu.VMEM) for x in operands]
    return in_order(
        functools.partial(strip_kernel, INSTANCES[name], height, group, names, pack),
        [jax.ShapeDtypeStruct(PACKED_SHAPE if pack else (height, sum(map(width_of, group))), F32)],
        [pltpu.with_memory_space_constraint(table, pltpu.SMEM), *pinned, *same, *half],
        [pltpu.SMEM] + [pltpu.VMEM] * (4 + len(names)),
        after,
        name=f"strip_{name}" + ("" if group == FULL else "_far" if group == FAR else "_near"),
    )[0]


def sum_kernel(group, *refs):
    *olds, came, out = refs
    if group == FAR:
        value = came[...]
        for ref in olds:
            value = value + ref[:, : out.shape[1]]
        out[...] = value
        return
    for k, r, c0, n, at in PACKED:
        value = came[:, at : at + n]
        for ref in olds:
            c = ref.shape[1] - 2 * TWO + near_column(k, c0)
            value = value + ref[r : r + SUB, c : c + n]
        out[:, at : at + n] = value


def add_up(name, group, after, came, *olds):
    return in_order(
        functools.partial(sum_kernel, group),
        [jax.ShapeDtypeStruct(came.shape, F32)],
        [*olds, came],
        [pltpu.VMEM] * (1 + len(olds)),
        after,
        name=name,
    )[0]


def total_far_kernel(table, a, b, c, d, own, four, *sends):
    core = pl.multiple_of(table[0, CORE], SUB)

    def add(rows, columns):
        return (a[rows, columns] + b[rows, columns]) + (c[rows, columns] + d[rows, columns])

    own[...] = add(pl.ds(core, SUB), slice(None))
    four[...] = own[:, 0:SUB]
    for out, at in zip(sends, (SUB, SUB + TWO)):
        out[...] = add(slice(None), pl.ds(pl.multiple_of(core + at, SUB), SUB))


def total_near_kernel(table, a, b, own, sent):
    core = pl.multiple_of(table[0, CORE], SUB)

    def add(at, n):
        columns = pl.ds(at, n)
        return a[:, columns] + b[:, columns]

    own[:, 0:TWO] = add(pl.multiple_of(2 * core, SUB), TWO)
    for r in range(2):
        sent[SUB * r : SUB * r + SUB, :] = add(pl.multiple_of(TWO * r + core, SUB), SUB)

    @pl.when(core == 0)
    def _():
        own[:, TWO:] = add(2 * TWO, TWO)

    @pl.when(core != 0)
    def _():
        own[:, TWO : TWO + SUB] = add(2 * TWO + SUB, SUB).T
        own[:, TWO + SUB :] = add(3 * TWO, SUB)


def total(group, table, after, *terms):
    blocks = [(SUB, sum(map(width_of, group)))]
    blocks += [(SUB, SUB), (TWO, SUB), (TWO, SUB)] if group == FAR else [(TWO, SUB)]
    return in_order(
        total_far_kernel if group == FAR else total_near_kernel,
        [jax.ShapeDtypeStruct(b, F32) for b in blocks],
        [pltpu.with_memory_space_constraint(table, pltpu.SMEM), *terms],
        [pltpu.SMEM] + [pltpu.VMEM] * len(terms),
        after,
        name="total_far" if group == FAR else "total_near",
    )


SENT = {K4A: 4, K3: 3, K2: 2, K1: 1}


def place_kernel(table, far, near, *refs):
    got, (out, turned, sems) = refs[: len(SENT)], refs[len(SENT) :]
    copies = []

    def put(entry, source):
        columns = pl.ds(pl.multiple_of(table[0, entry], SUB), source.shape[1])
        copy = pltpu.make_async_copy(source, out.at[:, columns], sems.at[len(copies)])
        copy.start()
        copies.append(copy)

    for group, own in ((FAR, far), (NEAR, near)):
        c = 0
        for k in group:
            put(FOUR if k == K4A else INSTANCES["5"] + k, own.at[:, c : c + width_of(k)])
            c += width_of(k)
    c = 0
    for k, ref in zip(SENT, got):
        w = ref.shape[0]
        turned[:, c : c + w] = ref[...].T
        put(R1 + SENT[k] - 1, turned.at[:, c : c + w])
        c += w
    for copy in copies:
        copy.wait()


def place(table, far, near, *got, order):
    return pl.pallas_call(
        place_kernel,
        out_shape=jax.ShapeDtypeStruct((SUB, order), F32),
        in_specs=[pl.BlockSpec(memory_space=pltpu.SMEM)]
        + [pl.BlockSpec(memory_space=pltpu.VMEM)] * (2 + len(got)),
        out_specs=pl.BlockSpec(memory_space=pl.ANY),
        scratch_shapes=[
            pltpu.VMEM((SUB, sum(g.shape[0] for g in got)), F32),
            pltpu.SemaphoreType.DMA((9,)),
        ],
        compiler_params=pltpu.CompilerParams(vmem_limit_bytes=20 * MIB),
        cost_estimate=pl.CostEstimate(flops=int(COST), bytes_accessed=0, transcendentals=0),
        name="place",
    )(pltpu.with_memory_space_constraint(table, pltpu.SMEM), far, near, *got)


def ring_gram(snapshots, block_of, mass_table, axis):
    rows, order = snapshots.shape
    ring, swap, fours = [], [], []
    far = {1: [], 2: [], 3: []}
    for p in range(CHIPS):
        for c in range(2):
            here = ring_device(p, c)
            ring.append((here, ring_device(p + 1 - 2 * c, c)))
            swap.append((here, ring_device(p, 1 - c)))
            fours.append((here, ring_device(p + 4, fourth(p, c))))
            for k in far:
                far[k].append((here, ring_device(pair(p, k), c)))
    places = jnp.asarray(position_table())
    *operands, table = prepare(snapshots, block_of, mass_table, 1.0 / (rows * 2 * CHIPS), places, axis)
    send = lambda x, pairs: lax.ppermute(x, axis, pairs)
    compute = lambda name, group, height, *rest, **adds: strip(
        name, group, height, operands, table, *rest, **adds
    )

    b = compute("1B", FULL, SUB, None)
    o = send(b, swap)
    last = compute("2B", FULL, TWO, b)
    o2 = send(last, swap)
    a_far = compute("1A", FAR, SUB, last, same=(o,))
    last = compute("1A", NEAR, SUB, a_far, same=(o,))
    r_far, r_near = send(a_far, ring), send(last, ring)
    o = o2
    for step in (2, 3, 4):
        if step < 4:
            last = b = compute(f"{step + 1}B", FULL, TWO, last)
        if step == 2:
            last = a_far = compute("2A", FAR, TWO, last, same=(o,), half=(r_far,))
            last = a_near = compute("2A", NEAR, TWO, last, same=(o,), half=(r_near,), pack=True)
        else:
            last = mine = compute(f"{step}A", FULL, TWO, last)
            last = a_far = add_up(f"sum_{step}_far", FAR, last, r_far, mine, o)
            if step == 4:
                last = b = compute("5", FAR, TWO, last)
            last = a_near = add_up(f"sum_{step}_near", NEAR, last, r_near, mine, o)
        r_far, r_near = send(a_far, ring), send(a_near, ring)
        o = send(b, swap)
    last = b_near = compute("5", NEAR, TWO, last)
    own_far, *sends = total(FAR, table, last, b, o, r_far, send(r_far, swap))
    got = [send(sends[0], fours), send(sends[1], far[3]), send(sends[2], far[2])]
    near = add_up("add_own", NEAR, own_far, r_near, b_near)
    own_near, sent = total(NEAR, table, None, near, send(near, swap))
    got_near = send(sent, far[1])
    return place(table, own_far, own_near, *got, got_near, order=order)


def scattered_gram(snapshots, block_of, mass_table, axis):
    rows, order = snapshots.shape
    scale = 1.0 / (rows * lax.axis_size(axis))
    places = jnp.zeros((lax.axis_size(axis), 1, 128), jnp.int32)
    xh, xl, wh, wl, _ = prepare(snapshots, block_of, mass_table, scale, places, axis)

    def dot(a, b):
        return lax.dot_general(a, b, (((0,), (0,)), ((), ())), preferred_element_type=F32)

    return lax.psum_scatter(
        dot(xh, wh) + (dot(xh, wl) + dot(xl, wh)), axis, scatter_dimension=0, tiled=True
    )


def per_device(snapshots, block_of, mass_table):
    axis = "space"
    ring = lax.axis_size(axis) == 2 * CHIPS and snapshots.shape[1] == 2 * CHIPS * SUB
    form = ring_gram if ring else scattered_gram
    return form(snapshots, block_of, mass_table, axis)


def solution(mesh):
    return jax.shard_map(
        per_device,
        mesh=mesh,
        in_specs=(P(("groups", "space"), None), P(("groups", "space")), P()),
        out_specs=P(("groups", "space"), None),
        check_vma=False,
    )
```

```python
import functools

import jax
import jax.numpy as jnp
import numpy as np
from jax import lax
from jax.experimental import pallas as pl
from jax.experimental.pallas import tpu as pltpu
from jax.sharding import PartitionSpec as P

F32 = jnp.float32
BF16 = jnp.bfloat16
MIB = 1 << 20
CHIPS = 8
SUB = 128
TWO = 2 * SUB


def prep_kernel(scale, axis, block_hbm, mass_hbm, x_hbm, places, xh, xl, wh, wl, place, x, table, both, block_of, mass, sems, small):
    rows, order = x_hbm.shape
    nodes, _, classes = mass.shape
    pairs = ((block_hbm, block_of), (mass_hbm, mass), (places.at[lax.axis_index(axis)], place))
    first = [pltpu.make_async_copy(a, b, small.at[i]) for i, (a, b) in enumerate(pairs)]
    for copy in first:
        copy.start()
    per_element = rows // block_of.shape[0]
    bands, _, band = both.shape
    wide = order // PIECES
    copies = []
    for b in range(bands):
        for h in range(PIECES):
            at = (pl.ds(b * band, band), pl.ds(h * wide, wide))
            copy = pltpu.make_async_copy(x_hbm.at[at], x.at[at], sems.at[PIECES * b + h])
            copy.start()
            copies.append(copy)
    for copy in first:
        copy.wait()
    row = lax.broadcasted_iota(jnp.int32, (8, band), 0)
    column = lax.broadcasted_iota(jnp.int32, (8, band), 1)
    here = [[(row % nodes == i) & (column % nodes == j) for j in range(nodes)] for i in range(nodes)]
    for k in range(classes):
        tile = jnp.zeros((8, band), F32)
        for i in range(nodes):
            for j in range(nodes):
                tile = jnp.where(here[i][j], mass[i, j, k] * scale, tile)
        table[8 * k : 8 * k + 8, :] = tile
    for b in range(bands):
        for g in range(0, band // 8, 2):
            tiles = []
            for e in (g, g + 1):
                kind = block_of[(b * band + 8 * e) // per_element]
                tile = table[pl.ds(pl.multiple_of(kind * 8, 8), 8), :]
                tiles.append(jnp.where((row + 8 * e) // nodes == column // nodes, tile, 0.0))
            tile = jnp.concatenate(tiles, axis=0)
            high = tile.astype(BF16)
            both[b, 8 * g : 8 * g + 16, :] = high
            both[b, band + 8 * g : band + 8 * g + 16, :] = (tile - high.astype(F32)).astype(BF16)
    dot = functools.partial(jnp.dot, preferred_element_type=F32)
    for b in range(bands):
        for h in range(PIECES):
            copies[PIECES * b + h].wait()
            at = (pl.ds(b * band, band), pl.ds(h * wide, wide))
            value = x[at]
            high = value.astype(BF16)
            low = (value - high.astype(F32)).astype(BF16)
            xh[at] = high
            xl[at] = low
            weighted = dot(both[b], high)
            weighted = weighted[:band] + weighted[band:] + dot(both[b, :band], low)
            high = weighted.astype(BF16)
            wh[at] = high
            wl[at] = (weighted - high.astype(F32)).astype(BF16)


PIECES = 1


def prepare(snapshots, block_of, mass_table, scale, places, axis):
    rows, order = snapshots.shape
    band = TWO
    bands = rows // band
    smem = pl.BlockSpec(memory_space=pltpu.SMEM)
    vmem = pl.BlockSpec(memory_space=pltpu.VMEM)
    return pl.pallas_call(
        functools.partial(prep_kernel, scale, axis),
        out_shape=[pltpu.VMEM((rows, order), BF16)] * 4 + [pltpu.SMEM(places.shape[1:], jnp.int32)],
        in_specs=[pl.BlockSpec(memory_space=pl.ANY)] * 4,
        out_specs=[vmem] * 4 + [smem],
        scratch_shapes=[
            pltpu.VMEM((rows, order), F32),
            pltpu.VMEM((8 * mass_table.shape[0], band), F32),
            pltpu.VMEM((bands, 2 * band, band), BF16),
            pltpu.SMEM(block_of.shape, jnp.int32),
            pltpu.SMEM(mass_table.shape[1:] + mass_table.shape[:1], F32),
            pltpu.SemaphoreType.DMA((PIECES * bands,)),
            pltpu.SemaphoreType.DMA((3,)),
        ],
        compiler_params=pltpu.CompilerParams(vmem_limit_bytes=32 * MIB),
        cost_estimate=pl.CostEstimate(
            flops=6 * rows * order * band, bytes_accessed=6 * rows * order, transcendentals=0
        ),
        name="weighting",
    )(*(pltpu.with_memory_space_constraint(x, pltpu.HBM) for x in (block_of, mass_table.transpose(1, 2, 0), snapshots, places)))


LHS, K0, K1, K2, K3, K4A, K4B = range(7)
FAR, NEAR = (K4A, K3, K2), (K1, K0)
FULL = FAR + NEAR
COST = 5000000000.0
COSTS = {"sum_4_far": 0.02, "sum_4_near": 10, "strip_5_far": 0.02, "strip_5_near": 3, "total_far": 0.1, "total_near": 0.02, "add_own": 0.02}
INSTANCES = {name: 7 * i for i, name in enumerate(("1A", "1B", "2A", "2B", "3A", "3B", "4A", "4B", "5"))}
CORE, R1, R2, R3, R4, FOUR = range(63, 69)


def ring_chip(p):
    p %= CHIPS
    return 2 * p if p < 4 else 2 * (CHIPS - 1 - p) + 1


def ring_device(p, core):
    return 2 * ring_chip(p) + core


PAIRS = ((7, 3, 0, 2, 5, 6, 4, 1), (5, 6, 4, 0, 1, 3, 7, 2), (1, 2, 5, 6, 3, 7, 0, 4))


def pair(q, k):
    return PAIRS[k - 1][q % CHIPS]


def fourth(q, r):
    return r if q % CHIPS < 4 else 1 - r


def position_table():
    table = np.zeros((2 * CHIPS, 1, 128), np.int32)

    def strip(q, half=None):
        at = TWO * ring_chip(q)
        cols = [TWO * ring_chip(pair(q, k) if k else q) for k in range(4)]
        fours = [TWO * ring_chip(q + 4) + SUB * fourth(q, r) for r in range(2)]
        if half is None:
            return [at] + cols + fours
        return [at + SUB * half] + cols + [fours[half]] * 2

    for p in range(CHIPS):
        for c in range(2):
            sign = 1 - 2 * c
            row = strip(p + 4, c) + strip(p + 4, 1 - c)
            for step in (2, 3, 4):
                row += strip(p + sign * (5 - step)) + strip(p - sign * (5 - step))
            row += strip(p)
            row += [SUB * c] + [TWO * ring_chip(q) for k in (1, 2, 3) for q in range(CHIPS) if pair(q, k) % CHIPS == p]
            row += [TWO * ring_chip(p + 4) + SUB * (c if (p + 4) % CHIPS < 4 else 1 - c)]
            row += [strip(p, c)[K4A]]
            table[ring_device(p, c), 0, : len(row)] = row
    return table


PACKED = ((K1, 0, 0, TWO, 0), (K1, SUB, 0, TWO, TWO), (K0, 0, 0, TWO, 2 * TWO), (K0, SUB, SUB, SUB, 3 * TWO))
PACKED_SHAPE = (SUB, 3 * TWO + SUB)


def near_column(k, c):
    return c if k == K1 else TWO + c


def width_of(k):
    return SUB if k == K4A else TWO


def in_order(kernel, out_shape, operands, spaces, after, name, **kwargs):
    if after is not None:
        operands, spaces = operands + [after], spaces + [pl.ANY]
        inner, count = kernel, len(operands)
        kernel = lambda *refs: inner(*refs[: count - 1], *refs[count:])
    outs = pl.pallas_call(
        kernel,
        out_shape=out_shape,
        in_specs=[pl.BlockSpec(memory_space=s) for s in spaces],
        out_specs=[pl.BlockSpec(memory_space=pltpu.VMEM)] * len(out_shape),
        compiler_params=pltpu.CompilerParams(vmem_limit_bytes=20 * MIB),
        cost_estimate=pl.CostEstimate(flops=int(COST * COSTS.get(name, 1)), bytes_accessed=0, transcendentals=0),
        name=name,
        **kwargs,
    )(*operands)
    return list(outs)


def strip_kernel(base, height, group, names, pack, table, xh, xl, wh, wl, *refs):
    ins, out = refs[:-1], refs[-1]
    width = sum(map(width_of, group))

    def entry(i):
        return pl.multiple_of(table[0, base + i], SUB)

    def dot(a, b):
        return jnp.dot(a, b, preferred_element_type=F32)

    rows = pl.ds(entry(LHS), height)
    ah, al = xh[:, rows].T, xl[:, rows].T
    c = 0
    for k in group:
        w = width_of(k)
        pieces = [(0, height, entry(k))]
        if k == K4A:
            pieces = [(SUB * r, SUB, entry(K4A + r)) for r in range(height // SUB)]
        for r, n, at in pieces:
            bh, bl = wh[:, pl.ds(at, w)], wl[:, pl.ds(at, w)]
            lh, ll = ah[r : r + n], al[r : r + n]
            value = dot(lh, bh) + dot(lh, bl) + dot(ll, bh)
            for name, ref in zip(names, ins):
                if name == "same":
                    c0 = ref.shape[1] - width + c if group == NEAR else c
                    value = value + ref[r : r + n, c0 : c0 + w]
            if not pack:
                out[r : r + n, c : c + w] = value
        if pack:
            for _, r, c0, n, at in (p for p in PACKED if p[0] == k):
                out[:, at : at + n] = value[r : r + SUB, c0 : c0 + n]
        c += w
    for name, ref in zip(names, ins):
        if name == "half" and pack:
            for mine in range(2):

                @pl.when(table[0, CORE] == SUB * mine)
                def _():
                    for k, r, c0, n, at in PACKED:
                        if r == SUB * mine:
                            c = near_column(k, c0)
                            out[:, at : at + n] = out[:, at : at + n] + ref[:, c : c + n]

        elif name == "half":
            rows = pl.ds(pl.multiple_of(table[0, CORE], SUB), SUB)
            out[rows, :] = out[rows, :] + ref[...]


def strip(name, group, height, operands, table, after, same=(), half=(), pack=False):
    names = ("same",) * len(same) + ("half",) * len(half)
    pinned = [pltpu.with_memory_space_constraint(x, pltpu.VMEM) for x in operands]
    return in_order(
        functools.partial(strip_kernel, INSTANCES[name], height, group, names, pack),
        [jax.ShapeDtypeStruct(PACKED_SHAPE if pack else (height, sum(map(width_of, group))), F32)],
        [pltpu.with_memory_space_constraint(table, pltpu.SMEM), *pinned, *same, *half],
        [pltpu.SMEM] + [pltpu.VMEM] * (4 + len(names)),
        after,
        name=f"strip_{name}" + ("" if group == FULL else "_far" if group == FAR else "_near"),
    )[0]


def sum_kernel(group, *refs):
    *olds, came, out = refs
    if group == FAR:
        value = came[...]
        for ref in olds:
            value = value + ref[:, : out.shape[1]]
        out[...] = value
        return
    for k, r, c0, n, at in PACKED:
        value = came[:, at : at + n]
        for ref in olds:
            c = ref.shape[1] - 2 * TWO + near_column(k, c0)
            value = value + ref[r : r + SUB, c : c + n]
        out[:, at : at + n] = value


def add_up(name, group, after, came, *olds):
    return in_order(
        functools.partial(sum_kernel, group),
        [jax.ShapeDtypeStruct(came.shape, F32)],
        [*olds, came],
        [pltpu.VMEM] * (1 + len(olds)),
        after,
        name=name,
    )[0]


def total_far_kernel(table, a, b, c, d, own, four, *sends):
    core = pl.multiple_of(table[0, CORE], SUB)

    def add(rows, columns):
        return (a[rows, columns] + b[rows, columns]) + (c[rows, columns] + d[rows, columns])

    own[...] = add(pl.ds(core, SUB), slice(None))
    four[...] = own[:, 0:SUB]
    for out, at in zip(sends, (SUB, SUB + TWO)):
        out[...] = add(slice(None), pl.ds(pl.multiple_of(core + at, SUB), SUB))


def total_near_kernel(table, a, b, own, sent):
    core = pl.multiple_of(table[0, CORE], SUB)

    def add(at, n):
        columns = pl.ds(at, n)
        return a[:, columns] + b[:, columns]

    own[:, 0:TWO] = add(pl.multiple_of(2 * core, SUB), TWO)
    for r in range(2):
        sent[SUB * r : SUB * r + SUB, :] = add(pl.multiple_of(TWO * r + core, SUB), SUB)

    @pl.when(core == 0)
    def _():
        own[:, TWO:] = add(2 * TWO, TWO)

    @pl.when(core != 0)
    def _():
        own[:, TWO : TWO + SUB] = add(2 * TWO + SUB, SUB).T
        own[:, TWO + SUB :] = add(3 * TWO, SUB)


def total(group, table, after, *terms):
    blocks = [(SUB, sum(map(width_of, group)))]
    blocks += [(SUB, SUB), (TWO, SUB), (TWO, SUB)] if group == FAR else [(TWO, SUB)]
    return in_order(
        total_far_kernel if group == FAR else total_near_kernel,
        [jax.ShapeDtypeStruct(b, F32) for b in blocks],
        [pltpu.with_memory_space_constraint(table, pltpu.SMEM), *terms],
        [pltpu.SMEM] + [pltpu.VMEM] * len(terms),
        after,
        name="total_far" if group == FAR else "total_near",
    )


SENT = {K4A: 4, K3: 3, K2: 2, K1: 1}


def place_kernel(table, far, near, *refs):
    got, (out, turned, sems) = refs[: len(SENT)], refs[len(SENT) :]
    copies = []

    def put(entry, source):
        columns = pl.ds(pl.multiple_of(table[0, entry], SUB), source.shape[1])
        copy = pltpu.make_async_copy(source, out.at[:, columns], sems.at[len(copies)])
        copy.start()
        copies.append(copy)

    for group, own in ((FAR, far), (NEAR, near)):
        c = 0
        for k in group:
            put(FOUR if k == K4A else INSTANCES["5"] + k, own.at[:, c : c + width_of(k)])
            c += width_of(k)
    c = 0
    for k, ref in zip(SENT, got):
        w = ref.shape[0]
        turned[:, c : c + w] = ref[...].T
        put(R1 + SENT[k] - 1, turned.at[:, c : c + w])
        c += w
    for copy in copies:
        copy.wait()


def place(table, far, near, *got, order):
    return pl.pallas_call(
        place_kernel,
        out_shape=jax.ShapeDtypeStruct((SUB, order), F32),
        in_specs=[pl.BlockSpec(memory_space=pltpu.SMEM)]
        + [pl.BlockSpec(memory_space=pltpu.VMEM)] * (2 + len(got)),
        out_specs=pl.BlockSpec(memory_space=pl.ANY),
        scratch_shapes=[
            pltpu.VMEM((SUB, sum(g.shape[0] for g in got)), F32),
            pltpu.SemaphoreType.DMA((9,)),
        ],
        compiler_params=pltpu.CompilerParams(vmem_limit_bytes=20 * MIB),
        cost_estimate=pl.CostEstimate(flops=int(COST), bytes_accessed=0, transcendentals=0),
        name="place",
    )(pltpu.with_memory_space_constraint(table, pltpu.SMEM), far, near, *got)


def ring_gram(snapshots, block_of, mass_table, axis):
    rows, order = snapshots.shape
    ring, swap, fours = [], [], []
    far = {1: [], 2: [], 3: []}
    for p in range(CHIPS):
        for c in range(2):
            here = ring_device(p, c)
            ring.append((here, ring_device(p + 1 - 2 * c, c)))
            swap.append((here, ring_device(p, 1 - c)))
            fours.append((here, ring_device(p + 4, fourth(p, c))))
            for k in far:
                far[k].append((here, ring_device(pair(p, k), c)))
    places = jnp.asarray(position_table())
    *operands, table = prepare(snapshots, block_of, mass_table, 1.0 / (rows * 2 * CHIPS), places, axis)
    send = lambda x, pairs: lax.ppermute(x, axis, pairs)
    compute = lambda name, group, height, *rest, **adds: strip(
        name, group, height, operands, table, *rest, **adds
    )

    b = compute("1B", FULL, SUB, None)
    o = send(b, swap)
    last = compute("2B", FULL, TWO, b)
    o2 = send(last, swap)
    a_far = compute("1A", FAR, SUB, last, same=(o,))
    last = compute("1A", NEAR, SUB, a_far, same=(o,))
    r_far, r_near = send(a_far, ring), send(last, ring)
    o = o2
    for step in (2, 3, 4):
        if step < 4:
            last = b = compute(f"{step + 1}B", FULL, TWO, last)
        if step == 2:
            last = a_far = compute("2A", FAR, TWO, last, same=(o,), half=(r_far,))
            last = a_near = compute("2A", NEAR, TWO, last, same=(o,), half=(r_near,), pack=True)
        else:
            last = mine = compute(f"{step}A", FULL, TWO, last)
            last = a_far = add_up(f"sum_{step}_far", FAR, last, r_far, mine, o)
            if step == 4:
                last = b = compute("5", FAR, TWO, last)
            last = a_near = add_up(f"sum_{step}_near", NEAR, last, r_near, mine, o)
        r_far, r_near = send(a_far, ring), send(a_near, ring)
        o = send(b, swap)
    last = b_near = compute("5", NEAR, TWO, last)
    own_far, *sends = total(FAR, table, last, b, o, r_far, send(r_far, swap))
    got = [send(sends[0], fours), send(sends[1], far[3]), send(sends[2], far[2])]
    near = add_up("add_own", NEAR, own_far, r_near, b_near)
    own_near, sent = total(NEAR, table, None, near, send(near, swap))
    got_near = send(sent, far[1])
    return place(table, own_far, own_near, *got, got_near, order=order)


def scattered_gram(snapshots, block_of, mass_table, axis):
    rows, order = snapshots.shape
    scale = 1.0 / (rows * lax.axis_size(axis))
    places = jnp.zeros((lax.axis_size(axis), 1, 128), jnp.int32)
    xh, xl, wh, wl, _ = prepare(snapshots, block_of, mass_table, scale, places, axis)

    def dot(a, b):
        return lax.dot_general(a, b, (((0,), (0,)), ((), ())), preferred_element_type=F32)

    return lax.psum_scatter(
        dot(xh, wh) + (dot(xh, wl) + dot(xl, wh)), axis, scatter_dimension=0, tiled=True
    )


def per_device(snapshots, block_of, mass_table):
    axis = "space"
    ring = lax.axis_size(axis) == 2 * CHIPS and snapshots.shape[1] == 2 * CHIPS * SUB
    form = ring_gram if ring else scattered_gram
    return form(snapshots, block_of, mass_table, axis)


def solution(mesh):
    return jax.shard_map(
        per_device,
        mesh=mesh,
        in_specs=(P(("groups", "space"), None), P(("groups", "space")), P()),
        out_specs=P(("groups", "space"), None),
        check_vma=False,
    )
```

```python
import functools

import jax
import jax.numpy as jnp
import numpy as np
from jax import lax
from jax.experimental import pallas as pl
from jax.experimental.pallas import tpu as pltpu
from jax.sharding import PartitionSpec as P

F32 = jnp.float32
BF16 = jnp.bfloat16
MIB = 1 << 20
CHIPS = 8
SUB = 128
TWO = 2 * SUB


def prep_kernel(scale, axis, block_hbm, mass_hbm, x_hbm, places, xh, xl, wh, wl, place, x, table, both, block_of, mass, sems, small):
    rows, order = x_hbm.shape
    nodes, _, classes = mass.shape
    pairs = ((block_hbm, block_of), (mass_hbm, mass), (places.at[lax.axis_index(axis)], place))
    first = [pltpu.make_async_copy(a, b, small.at[i]) for i, (a, b) in enumerate(pairs)]
    for copy in first:
        copy.start()
    per_element = rows // block_of.shape[0]
    bands, _, band = both.shape
    wide = order // PIECES
    copies = []
    for b in range(bands):
        for h in range(PIECES):
            at = (pl.ds(b * band, band), pl.ds(h * wide, wide))
            copy = pltpu.make_async_copy(x_hbm.at[at], x.at[at], sems.at[PIECES * b + h])
            copy.start()
            copies.append(copy)
    for copy in first:
        copy.wait()
    row = lax.broadcasted_iota(jnp.int32, (8, band), 0)
    column = lax.broadcasted_iota(jnp.int32, (8, band), 1)
    here = [[(row % nodes == i) & (column % nodes == j) for j in range(nodes)] for i in range(nodes)]
    for k in range(classes):
        tile = jnp.zeros((8, band), F32)
        for i in range(nodes):
            for j in range(nodes):
                tile = jnp.where(here[i][j], mass[i, j, k] * scale, tile)
        table[8 * k : 8 * k + 8, :] = tile
    for b in range(bands):
        for g in range(0, band // 8, 2):
            tiles = []
            for e in (g, g + 1):
                kind = block_of[(b * band + 8 * e) // per_element]
                tile = table[pl.ds(pl.multiple_of(kind * 8, 8), 8), :]
                tiles.append(jnp.where((row + 8 * e) // nodes == column // nodes, tile, 0.0))
            tile = jnp.concatenate(tiles, axis=0)
            high = tile.astype(BF16)
            both[b, 8 * g : 8 * g + 16, :] = high
            both[b, band + 8 * g : band + 8 * g + 16, :] = (tile - high.astype(F32)).astype(BF16)
    dot = functools.partial(jnp.dot, preferred_element_type=F32)
    for b in range(bands):
        for h in range(PIECES):
            copies[PIECES * b + h].wait()
            at = (pl.ds(b * band, band), pl.ds(h * wide, wide))
            value = x[at]
            high = value.astype(BF16)
            low = (value - high.astype(F32)).astype(BF16)
            xh[at] = high
            xl[at] = low
            mh, ml = both[b, :band], both[b, band:]
            weighted = dot(mh, high) + dot(ml, high) + dot(mh, low)
            high = weighted.astype(BF16)
            wh[at] = high
            wl[at] = (weighted - high.astype(F32)).astype(BF16)


PIECES = 1


def prepare(snapshots, block_of, mass_table, scale, places, axis):
    rows, order = snapshots.shape
    band = TWO
    bands = rows // band
    smem = pl.BlockSpec(memory_space=pltpu.SMEM)
    vmem = pl.BlockSpec(memory_space=pltpu.VMEM)
    return pl.pallas_call(
        functools.partial(prep_kernel, scale, axis),
        out_shape=[pltpu.VMEM((rows, order), BF16)] * 4 + [pltpu.SMEM(places.shape[1:], jnp.int32)],
        in_specs=[pl.BlockSpec(memory_space=pl.ANY)] * 4,
        out_specs=[vmem] * 4 + [smem],
        scratch_shapes=[
            pltpu.VMEM((rows, order), F32),
            pltpu.VMEM((8 * mass_table.shape[0], band), F32),
            pltpu.VMEM((bands, 2 * band, band), BF16),
            pltpu.SMEM(block_of.shape, jnp.int32),
            pltpu.SMEM(mass_table.shape[1:] + mass_table.shape[:1], F32),
            pltpu.SemaphoreType.DMA((PIECES * bands,)),
            pltpu.SemaphoreType.DMA((3,)),
        ],
        compiler_params=pltpu.CompilerParams(vmem_limit_bytes=32 * MIB),
        cost_estimate=pl.CostEstimate(
            flops=6 * rows * order * band, bytes_accessed=6 * rows * order, transcendentals=0
        ),
        name="weighting",
    )(*(pltpu.with_memory_space_constraint(x, pltpu.HBM) for x in (block_of, mass_table.transpose(1, 2, 0), snapshots, places)))


LHS, K0, K1, K2, K3, K4A, K4B = range(7)
FAR, NEAR = (K4A, K3, K2), (K1, K0)
FULL = FAR + NEAR
COST = 5000000000.0
COSTS = {"sum_4_far": 0.02, "sum_4_near": 10, "strip_5_far": 0.02, "strip_5_near": 3, "total_far": 0.1, "total_near": 0.02, "add_own": 0.02}
INSTANCES = {name: 7 * i for i, name in enumerate(("1A", "1B", "2A", "2B", "3A", "3B", "4A", "4B", "5"))}
CORE, R1, R2, R3, R4, FOUR = range(63, 69)


def ring_chip(p):
    p %= CHIPS
    return 2 * p if p < 4 else 2 * (CHIPS - 1 - p) + 1


def ring_device(p, core):
    return 2 * ring_chip(p) + core


PAIRS = ((7, 3, 0, 2, 5, 6, 4, 1), (1, 2, 5, 6, 3, 7, 0, 4), (5, 6, 4, 0, 1, 3, 7, 2))


def pair(q, k):
    return PAIRS[k - 1][q % CHIPS]


def fourth(q, r):
    return r if q % CHIPS < 4 else 1 - r


def position_table():
    table = np.zeros((2 * CHIPS, 1, 128), np.int32)

    def strip(q, half=None):
        at = TWO * ring_chip(q)
        cols = [TWO * ring_chip(pair(q, k) if k else q) for k in range(4)]
        fours = [TWO * ring_chip(q + 4) + SUB * fourth(q, r) for r in range(2)]
        if half is None:
            return [at] + cols + fours
        return [at + SUB * half] + cols + [fours[half]] * 2

    for p in range(CHIPS):
        for c in range(2):
            sign = 1 - 2 * c
            row = strip(p + 4, c) + strip(p + 4, 1 - c)
            for step in (2, 3, 4):
                row += strip(p + sign * (5 - step)) + strip(p - sign * (5 - step))
            row += strip(p)
            row += [SUB * c] + [TWO * ring_chip(q) for k in (1, 2, 3) for q in range(CHIPS) if pair(q, k) % CHIPS == p]
            row += [TWO * ring_chip(p + 4) + SUB * (c if (p + 4) % CHIPS < 4 else 1 - c)]
            row += [strip(p, c)[K4A]]
            table[ring_device(p, c), 0, : len(row)] = row
    return table


PACKED = ((K1, 0, 0, TWO, 0), (K1, SUB, 0, TWO, TWO), (K0, 0, 0, TWO, 2 * TWO), (K0, SUB, SUB, SUB, 3 * TWO))
PACKED_SHAPE = (SUB, 3 * TWO + SUB)


def near_column(k, c):
    return c if k == K1 else TWO + c


def width_of(k):
    return SUB if k == K4A else TWO


def in_order(kernel, out_shape, operands, spaces, after, name, **kwargs):
    if after is not None:
        operands, spaces = operands + [after], spaces + [pl.ANY]
        inner, count = kernel, len(operands)
        kernel = lambda *refs: inner(*refs[: count - 1], *refs[count:])
    outs = pl.pallas_call(
        kernel,
        out_shape=out_shape,
        in_specs=[pl.BlockSpec(memory_space=s) for s in spaces],
        out_specs=[pl.BlockSpec(memory_space=pltpu.VMEM)] * len(out_shape),
        compiler_params=pltpu.CompilerParams(vmem_limit_bytes=20 * MIB),
        cost_estimate=pl.CostEstimate(flops=int(COST * COSTS.get(name, 1)), bytes_accessed=0, transcendentals=0),
        name=name,
        **kwargs,
    )(*operands)
    return list(outs)


def strip_kernel(base, height, group, names, pack, table, xh, xl, wh, wl, *refs):
    ins, out = refs[:-1], refs[-1]
    width = sum(map(width_of, group))

    def entry(i):
        return pl.multiple_of(table[0, base + i], SUB)

    def dot(a, b):
        return jnp.dot(a, b, preferred_element_type=F32)

    rows = pl.ds(entry(LHS), height)
    ah, al = xh[:, rows].T, xl[:, rows].T
    c = 0
    for k in group:
        w = width_of(k)
        pieces = [(0, height, entry(k))]
        if k == K4A:
            pieces = [(SUB * r, SUB, entry(K4A + r)) for r in range(height // SUB)]
        for r, n, at in pieces:
            bh, bl = wh[:, pl.ds(at, w)], wl[:, pl.ds(at, w)]
            lh, ll = ah[r : r + n], al[r : r + n]
            value = dot(lh, bh) + dot(lh, bl) + dot(ll, bh)
            for name, ref in zip(names, ins):
                if name == "same":
                    c0 = ref.shape[1] - width + c if group == NEAR else c
                    value = value + ref[r : r + n, c0 : c0 + w]
            if not pack:
                out[r : r + n, c : c + w] = value
        if pack:
            for _, r, c0, n, at in (p for p in PACKED if p[0] == k):
                out[:, at : at + n] = value[r : r + SUB, c0 : c0 + n]
        c += w
    for name, ref in zip(names, ins):
        if name == "half" and pack:
            for mine in range(2):

                @pl.when(table[0, CORE] == SUB * mine)
                def _():
                    for k, r, c0, n, at in PACKED:
                        if r == SUB * mine:
                            c = near_column(k, c0)
                            out[:, at : at + n] = out[:, at : at + n] + ref[:, c : c + n]

        elif name == "half":
            rows = pl.ds(pl.multiple_of(table[0, CORE], SUB), SUB)
            out[rows, :] = out[rows, :] + ref[...]


def strip(name, group, height, operands, table, after, same=(), half=(), pack=False):
    names = ("same",) * len(same) + ("half",) * len(half)
    pinned = [pltpu.with_memory_space_constraint(x, pltpu.VMEM) for x in operands]
    return in_order(
        functools.partial(strip_kernel, INSTANCES[name], height, group, names, pack),
        [jax.ShapeDtypeStruct(PACKED_SHAPE if pack else (height, sum(map(width_of, group))), F32)],
        [pltpu.with_memory_space_constraint(table, pltpu.SMEM), *pinned, *same, *half],
        [pltpu.SMEM] + [pltpu.VMEM] * (4 + len(names)),
        after,
        name=f"strip_{name}" + ("" if group == FULL else "_far" if group == FAR else "_near"),
    )[0]


def sum_kernel(group, *refs):
    *olds, came, out = refs
    if group == FAR:
        value = came[...]
        for ref in olds:
            value = value + ref[:, : out.shape[1]]
        out[...] = value
        return
    for k, r, c0, n, at in PACKED:
        value = came[:, at : at + n]
        for ref in olds:
            c = ref.shape[1] - 2 * TWO + near_column(k, c0)
            value = value + ref[r : r + SUB, c : c + n]
        out[:, at : at + n] = value


def add_up(name, group, after, came, *olds):
    return in_order(
        functools.partial(sum_kernel, group),
        [jax.ShapeDtypeStruct(came.shape, F32)],
        [*olds, came],
        [pltpu.VMEM] * (1 + len(olds)),
        after,
        name=name,
    )[0]


def total_far_kernel(table, a, b, c, d, own, four, *sends):
    core = pl.multiple_of(table[0, CORE], SUB)

    def add(rows, columns):
        return (a[rows, columns] + b[rows, columns]) + (c[rows, columns] + d[rows, columns])

    own[...] = add(pl.ds(core, SUB), slice(None))
    four[...] = own[:, 0:SUB]
    for out, at in zip(sends, (SUB, SUB + TWO)):
        out[...] = add(slice(None), pl.ds(pl.multiple_of(core + at, SUB), SUB))


def total_near_kernel(table, a, b, own, sent):
    core = pl.multiple_of(table[0, CORE], SUB)

    def add(at, n):
        columns = pl.ds(at, n)
        return a[:, columns] + b[:, columns]

    own[:, 0:TWO] = add(pl.multiple_of(2 * core, SUB), TWO)
    for r in range(2):
        sent[SUB * r : SUB * r + SUB, :] = add(pl.multiple_of(TWO * r + core, SUB), SUB)

    @pl.when(core == 0)
    def _():
        own[:, TWO:] = add(2 * TWO, TWO)

    @pl.when(core != 0)
    def _():
        own[:, TWO : TWO + SUB] = add(2 * TWO + SUB, SUB).T
        own[:, TWO + SUB :] = add(3 * TWO, SUB)


def total(group, table, after, *terms):
    blocks = [(SUB, sum(map(width_of, group)))]
    blocks += [(SUB, SUB), (TWO, SUB), (TWO, SUB)] if group == FAR else [(TWO, SUB)]
    return in_order(
        total_far_kernel if group == FAR else total_near_kernel,
        [jax.ShapeDtypeStruct(b, F32) for b in blocks],
        [pltpu.with_memory_space_constraint(table, pltpu.SMEM), *terms],
        [pltpu.SMEM] + [pltpu.VMEM] * len(terms),
        after,
        name="total_far" if group == FAR else "total_near",
    )


SENT = {K4A: 4, K3: 3, K2: 2, K1: 1}


def place_kernel(table, far, near, *refs):
    got, (out, turned, sems) = refs[: len(SENT)], refs[len(SENT) :]
    copies = []

    def put(entry, source):
        columns = pl.ds(pl.multiple_of(table[0, entry], SUB), source.shape[1])
        copy = pltpu.make_async_copy(source, out.at[:, columns], sems.at[len(copies)])
        copy.start()
        copies.append(copy)

    for group, own in ((FAR, far), (NEAR, near)):
        c = 0
        for k in group:
            put(FOUR if k == K4A else INSTANCES["5"] + k, own.at[:, c : c + width_of(k)])
            c += width_of(k)
    c = 0
    for k, ref in zip(SENT, got):
        w = ref.shape[0]
        turned[:, c : c + w] = ref[...].T
        put(R1 + SENT[k] - 1, turned.at[:, c : c + w])
        c += w
    for copy in copies:
        copy.wait()


def place(table, far, near, *got, order):
    return pl.pallas_call(
        place_kernel,
        out_shape=jax.ShapeDtypeStruct((SUB, order), F32),
        in_specs=[pl.BlockSpec(memory_space=pltpu.SMEM)]
        + [pl.BlockSpec(memory_space=pltpu.VMEM)] * (2 + len(got)),
        out_specs=pl.BlockSpec(memory_space=pl.ANY),
        scratch_shapes=[
            pltpu.VMEM((SUB, sum(g.shape[0] for g in got)), F32),
            pltpu.SemaphoreType.DMA((9,)),
        ],
        compiler_params=pltpu.CompilerParams(vmem_limit_bytes=20 * MIB),
        cost_estimate=pl.CostEstimate(flops=int(COST), bytes_accessed=0, transcendentals=0),
        name="place",
    )(pltpu.with_memory_space_constraint(table, pltpu.SMEM), far, near, *got)


def ring_gram(snapshots, block_of, mass_table, axis):
    rows, order = snapshots.shape
    ring, swap, fours = [], [], []
    far = {1: [], 2: [], 3: []}
    for p in range(CHIPS):
        for c in range(2):
            here = ring_device(p, c)
            ring.append((here, ring_device(p + 1 - 2 * c, c)))
            swap.append((here, ring_device(p, 1 - c)))
            fours.append((here, ring_device(p + 4, fourth(p, c))))
            for k in far:
                far[k].append((here, ring_device(pair(p, k), c)))
    places = jnp.asarray(position_table())
    *operands, table = prepare(snapshots, block_of, mass_table, 1.0 / (rows * 2 * CHIPS), places, axis)
    send = lambda x, pairs: lax.ppermute(x, axis, pairs)
    compute = lambda name, group, height, *rest, **adds: strip(
        name, group, height, operands, table, *rest, **adds
    )

    b = compute("1B", FULL, SUB, None)
    o = send(b, swap)
    last = compute("2B", FULL, TWO, b)
    o2 = send(last, swap)
    a_far = compute("1A", FAR, SUB, last, same=(o,))
    last = compute("1A", NEAR, SUB, a_far, same=(o,))
    r_far, r_near = send(a_far, ring), send(last, ring)
    o = o2
    for step in (2, 3, 4):
        if step < 4:
            last = b = compute(f"{step + 1}B", FULL, TWO, last)
        if step == 2:
            last = a_far = compute("2A", FAR, TWO, last, same=(o,), half=(r_far,))
            last = a_near = compute("2A", NEAR, TWO, last, same=(o,), half=(r_near,), pack=True)
        else:
            last = mine = compute(f"{step}A", FULL, TWO, last)
            last = a_far = add_up(f"sum_{step}_far", FAR, last, r_far, mine, o)
            if step == 4:
                last = b = compute("5", FAR, TWO, last)
            last = a_near = add_up(f"sum_{step}_near", NEAR, last, r_near, mine, o)
        r_far, r_near = send(a_far, ring), send(a_near, ring)
        o = send(b, swap)
    last = b_near = compute("5", NEAR, TWO, last)
    own_far, *sends = total(FAR, table, last, b, o, r_far, send(r_far, swap))
    got = [send(sends[0], fours), send(sends[1], far[3]), send(sends[2], far[2])]
    near = add_up("add_own", NEAR, own_far, r_near, b_near)
    own_near, sent = total(NEAR, table, None, near, send(near, swap))
    got_near = send(sent, far[1])
    return place(table, own_far, own_near, *got, got_near, order=order)


def scattered_gram(snapshots, block_of, mass_table, axis):
    rows, order = snapshots.shape
    scale = 1.0 / (rows * lax.axis_size(axis))
    places = jnp.zeros((lax.axis_size(axis), 1, 128), jnp.int32)
    xh, xl, wh, wl, _ = prepare(snapshots, block_of, mass_table, scale, places, axis)

    def dot(a, b):
        return lax.dot_general(a, b, (((0,), (0,)), ((), ())), preferred_element_type=F32)

    return lax.psum_scatter(
        dot(xh, wh) + (dot(xh, wl) + dot(xl, wh)), axis, scatter_dimension=0, tiled=True
    )


def per_device(snapshots, block_of, mass_table):
    axis = "space"
    ring = lax.axis_size(axis) == 2 * CHIPS and snapshots.shape[1] == 2 * CHIPS * SUB
    form = ring_gram if ring else scattered_gram
    return form(snapshots, block_of, mass_table, axis)


def solution(mesh):
    return jax.shard_map(
        per_device,
        mesh=mesh,
        in_specs=(P(("groups", "space"), None), P(("groups", "space")), P()),
        out_specs=P(("groups", "space"), None),
        check_vma=False,
    )
```
